32 devices in a mesh: gx: 2 (over x), gy: 4 (over y, core), gz: 4 (over z).
Axes of the slice: x: 2, y: 2, z: 4, core: 2. Of those that a mesh axis runs over, the one named last changes fastest.
Arguments:
- pre_act: bfloat16 [512, 24576], P('gx', ('gy', 'gz')), may hold values from -6 to 6
- grad_out: bfloat16 [512, 6144], P(('gx', 'gy'), 'gz'), may hold values from -0.625 to 0.625
- weight: bfloat16 [12288, 2, 6144], P('gy', 'gx', 'gz'), may hold values from -4 to 4
Outputs:
- pre_grad: bfloat16 [512, 24576], P('gx', ('gy', 'gz'))
- weight_grad: bfloat16 [12288, 2, 6144], P('gy', 'gx', 'gz')
The draws below stay inside these ranges and needn't reach their ends.
All inputs are finite; a program needn't handle non-finite values.
Results may differ from the reference program's by a relative error of at most 0.02.
Values may be sent and summed in bfloat16 or wider, within the bound.
A program may use at most 128 MiB of HBM per device.

```python
import jax
import jax.numpy as jnp
from jax import lax

DMODEL = 6144
FFN = 24576
TOK_DEV = 256
TOKENS = 512
N_GX = 2
N_GZ = 4


def level_of(stream_key, shape, shards, least, high):
    def one(dim, shards_of):
        steps = jax.random.uniform(jax.random.fold_in(jax.random.fold_in(stream_key, 6), dim), (shards_of,), jnp.float32, least / len(shards), high / len(shards))
        return jnp.repeat(jnp.exp(steps), shape[dim] // shards_of).reshape((-1,) + (1,) * (len(shape) - dim - 1))

    factor_of = one(*shards[0])
    for cut in shards[1:]:
        factor_of = factor_of * one(*cut)
    return factor_of


def normal_values(own_key, dims, scale, reach, pieces=(), dtype=jnp.bfloat16):
    array = scale * jax.random.normal(own_key, dims, jnp.float32)
    if pieces:
        array = array * level_of(own_key, dims, pieces, -0.22, 0.18)
    return jnp.clip(array, -reach, reach).astype(dtype)


def setup_inputs(seed: int = 0) -> dict:
    seeds = jax.random.split(jax.random.key(seed), 4)
    return {
        "pre_act": normal_values(seeds[0], (TOKENS, FFN), 1.0, 6.0, ((0, 2), (1, 16))),
        "grad_out": normal_values(seeds[1], (TOKENS, DMODEL), (TOKENS ** -0.5), 0.625, ((0, 8), (1, 4))),
        "weight": normal_values(seeds[2], (FFN // N_GX, N_GX, DMODEL), (TOKENS ** 0.5 * DMODEL ** -0.5), 4.0, ((0, 4), (1, 2), (2, 4))),
    }


tanh_scale = 0.7978845608028654
cubic_coef = 0.044715


def gelu_parts(inputs):
    inner = tanh_scale * (inputs + cubic_coef * inputs * inputs * inputs)
    tangent = jnp.tanh(inner)
    gelu_value = 0.5 * inputs * (1.0 + tangent)
    gelu_slope = 0.5 * (1.0 + tangent) + 0.5 * inputs * (1.0 - tangent * tangent) * tanh_scale * (1.0 + 3.0 * cubic_coef * inputs * inputs)
    return gelu_value, gelu_slope


def reference(pre_act, grad_out, weight):
    weight_flat = weight.reshape(FFN, DMODEL)
    gelu_value, gelu_slope = gelu_parts(pre_act.astype(jnp.float32))
    hidden = gelu_value.astype(jnp.bfloat16)
    width_block = DMODEL // N_GZ

    def add_width(block_index, running):
        offset = jnp.asarray(block_index, jnp.int32) * width_block
        grad_cols = lax.dynamic_slice_in_dim(grad_out, offset, width_block, 1)
        weight_cols = lax.dynamic_slice_in_dim(weight_flat, offset, width_block, 1)
        partial_block = lax.dot_general(grad_cols, weight_cols, (((1,), (1,)), ((), ())), preferred_element_type=jnp.float32)
        partial_block = lax.optimization_barrier(partial_block.astype(jnp.bfloat16))
        return running + partial_block.astype(jnp.float32)

    summed = lax.fori_loop(0, N_GZ, add_width, jnp.zeros((TOKENS, FFN), jnp.float32))
    pre_grad = (summed * gelu_slope).astype(jnp.bfloat16)

    def add_tokens(block_index, running):
        offset = jnp.asarray(block_index, jnp.int32) * TOK_DEV
        hidden_rows = lax.dynamic_slice_in_dim(hidden, offset, TOK_DEV, 0)
        grad_rows = lax.dynamic_slice_in_dim(grad_out, offset, TOK_DEV, 0)
        partial_block = lax.dot_general(hidden_rows, grad_rows, (((0,), (0,)), ((), ())), preferred_element_type=jnp.float32)
        partial_block = lax.optimization_barrier(partial_block.astype(jnp.bfloat16))
        return running + partial_block.astype(jnp.float32)

    weight_sum = lax.fori_loop(0, N_GX, add_tokens, jnp.zeros((FFN, DMODEL), jnp.float32))
    weight_grad = weight_sum.astype(jnp.bfloat16).reshape(FFN // N_GX, N_GX, DMODEL)
    return pre_grad, weight_grad
```

```python
import jax
import jax.numpy as jnp
from jax import lax
from jax.sharding import PartitionSpec as P

tanh_scale = 0.7978845608028654
cubic_coef = 0.044715


def gelu_parts(inputs):
    inner = tanh_scale * (inputs + cubic_coef * inputs * inputs * inputs)
    tangent = jnp.tanh(inner)
    gelu_value = 0.5 * inputs * (1.0 + tangent)
    gelu_slope = 0.5 * (1.0 + tangent) + 0.5 * inputs * (1.0 - tangent * tangent) * tanh_scale * (
        1.0 + 3.0 * cubic_coef * inputs * inputs
    )
    return (gelu_value, gelu_slope)


def per_device(pre_act, grad_out, weight):
    groups = lax.axis_size("gx")
    tokens, cols = pre_act.shape
    value, slope = gelu_parts(pre_act.astype(jnp.float32))
    split = value.astype(jnp.bfloat16).reshape(tokens, cols // groups, groups).transpose(2, 0, 1)
    hidden = lax.all_to_all(split, "gx", 0, 0, tiled=True)
    hidden = lax.all_gather(hidden, "gz", axis=2, tiled=True)
    hidden = hidden.reshape(groups * tokens, -1)
    grad_rows = lax.all_gather(grad_out, ("gx", "gy"), axis=0, tiled=True)
    partial = jnp.einsum("pd,rd->pr", grad_rows, weight[:, 0, :], preferred_element_type=jnp.float32)
    summed = lax.psum_scatter(partial.astype(jnp.bfloat16), "gz", scatter_dimension=1, tiled=True)
    summed = lax.all_to_all(summed.reshape(groups, tokens, -1), "gx", 0, 0, tiled=True)
    summed = summed.transpose(1, 2, 0).reshape(tokens, cols).astype(jnp.float32)
    pre_grad = (summed * slope).astype(jnp.bfloat16)
    weight_grad = jnp.einsum("pr,pd->rd", hidden, grad_rows, preferred_element_type=jnp.float32)
    return (pre_grad, weight_grad.astype(jnp.bfloat16)[:, None, :])


def solution(mesh):
    placed = (P("gx", ("gy", "gz")), P(("gx", "gy"), "gz"), P("gy", "gx", "gz"))
    return jax.shard_map(
        per_device,
        mesh=mesh,
        in_specs=placed,
        out_specs=(P("gx", ("gy", "gz")), P("gy", "gx", "gz")),
        check_vma=False,
    )
```

```python
import functools

import jax
import jax.numpy as jnp
from jax import lax
from jax.experimental import pallas as pl
from jax.experimental.pallas import tpu as pltpu
from jax.sharding import PartitionSpec as P

tanh_scale = 0.7978845608028654
cubic_coef = 0.044715
MESH = pl.DeviceIdType.MESH
UP, DOWN = 0, 1


def gelu_parts(inputs):
    inner = tanh_scale * (inputs + cubic_coef * inputs * inputs * inputs)
    tangent = jnp.tanh(inner)
    gelu_value = 0.5 * inputs * (1.0 + tangent)
    gelu_slope = 0.5 * (1.0 + tangent) + 0.5 * inputs * (1.0 - tangent * tangent) * tanh_scale * (
        1.0 + 3.0 * cubic_coef * inputs * inputs
    )
    return (gelu_value, gelu_slope)


def pick(me, values):
    out = jnp.int32(values[0])
    for at in range(1, len(values)):
        out = jnp.where(me == at, jnp.int32(values[at]), out)
    return out


def exchange_kernel(
    pre_ref,
    grad_ref,
    weight_ref,
    pre_grad_ref,
    hidden_ref,
    rows_ref,
    weight_vmem,
    rows,
    split,
    slope,
    part,
    arrived,
    outgoing,
    final,
    weight_sem,
    store_sem,
    grad_send,
    grad_recv,
    x_send,
    x_recv,
    ag_send,
    ag_recv,
    rs_send,
    rs_recv,
):
    gx, gy, me = lax.axis_index("gx"), lax.axis_index("gy"), lax.axis_index("gz")
    other_x = 1 - gx
    core = gy + 1 - 2 * lax.rem(gy, 2)
    far_y = lax.rem(gy + 2, 4)
    is_mid = jnp.logical_and(me > 0, me < 3)
    is_end = jnp.logical_not(is_mid)
    tokens, cols = pre_ref.shape
    block = grad_ref.shape[0]
    width = grad_ref.shape[1]
    units = cols // 2

    barrier = pltpu.get_barrier_semaphore()
    for peer in ({"gy": core}, {"gx": other_x}, {"gy": far_y}):
        pl.semaphore_signal(barrier, inc=1, device_id=peer, device_id_type=MESH)

    @pl.when(me > 0)
    def _():
        pl.semaphore_signal(barrier, inc=1, device_id={"gz": me - 1}, device_id_type=MESH)

    @pl.when(me < 3)
    def _():
        pl.semaphore_signal(barrier, inc=1, device_id={"gz": me + 1}, device_id_type=MESH)

    weight_load = pltpu.make_async_copy(weight_ref, weight_vmem, weight_sem)
    weight_load.start()
    pl.semaphore_wait(barrier, jnp.where(is_mid, 5, 4))

    def grad_copy(kind, bx, by, peer, src=None):
        at = rows.at[bx, pl.ds(pl.multiple_of(by * block, block), block), :]
        return pltpu.make_async_remote_copy(
            src_ref=at if src is None else src,
            dst_ref=at,
            send_sem=grad_send.at[kind],
            recv_sem=grad_recv.at[kind],
            device_id=peer,
            device_id_type=MESH,
        )

    to_x = grad_copy(1, gx, gy, {"gx": other_x}, grad_ref)
    to_y = grad_copy(2, gx, gy, {"gy": far_y}, grad_ref)
    to_core = grad_copy(0, gx, gy, {"gy": core}, grad_ref)
    to_x.start()
    to_y.start()
    to_core.start()
    rows[gx, pl.ds(pl.multiple_of(gy * block, block), block), :] = grad_ref[...]

    group = 256
    half = group // 2
    line = lax.broadcasted_iota(jnp.int32, (group, group), 0)
    lane = lax.broadcasted_iota(jnp.int32, (group, group), 1)
    target = jnp.where(line < half, 2 * line, 2 * (line - half) + 1)
    select = jnp.where(lane == target, 1.0, 0.0).astype(jnp.bfloat16)
    for q in range(cols // group):
        span = slice(q * group, (q + 1) * group)
        value, slope_part = gelu_parts(pre_ref[:, span].astype(jnp.float32))
        slope[:, span] = slope_part
        moved = lax.dot_general(
            select,
            value.astype(jnp.bfloat16),
            (((1,), (1,)), ((), ())),
            preferred_element_type=jnp.float32,
        ).astype(jnp.bfloat16)
        split[0, q * half : (q + 1) * half, :] = moved[:half]
        split[1, q * half : (q + 1) * half, :] = moved[half:]

    def remote(src, dst, send, recv, peer):
        return pltpu.make_async_remote_copy(
            src_ref=src,
            dst_ref=dst,
            send_sem=send,
            recv_sem=recv,
            device_id=peer,
            device_id_type=MESH,
        )

    def ag(way, second, hop):
        step = 1 - 2 * way
        owner = me - hop * step
        tok = other_x if second else gx
        at = hidden_ref.at[tok, owner]
        src = split.at[gx] if hop == 0 and not second else at
        return remote(src, at, ag_send.at[way, second, hop], ag_recv.at[way, second, hop], {"gz": me + step})

    def ag_arrival(way, second, hop):
        step = 1 - 2 * way
        owner = me - step - hop * step
        tok = other_x if second else gx
        at = hidden_ref.at[tok, owner]
        return remote(at, at, ag_send.at[way, second, hop], ag_recv.at[way, second, hop], {"gz": me - step})

    def both_ways(second):
        @pl.when(me < 3)
        def _():
            ag(UP, second, 0).start()

        @pl.when(me > 0)
        def _():
            ag(DOWN, second, 0).start()

    x_hidden = remote(split.at[other_x], hidden_ref.at[gx, me], x_send.at[0], x_recv.at[0], {"gx": other_x})
    x_hidden_in = remote(split.at[other_x], hidden_ref.at[other_x, me], x_send.at[0], x_recv.at[0], {"gx": other_x})
    x_hidden.start()
    both_ways(0)
    own_store = pltpu.make_async_copy(split.at[gx], hidden_ref.at[gx, me], store_sem.at[0])
    own_store.start()

    to_x.wait_recv()
    x_to_y = grad_copy(3, other_x, gy, {"gy": far_y})
    x_to_y.start()
    x_to_core = grad_copy(4, other_x, gy, {"gy": core})
    x_to_core.start()
    to_y.wait_recv()
    y_to_core = grad_copy(5, gx, far_y, {"gy": core})
    y_to_core.start()
    x_to_y.wait_recv()
    diag_to_core = grad_copy(6, other_x, far_y, {"gy": core})
    diag_to_core.start()
    for copy in (to_core, x_to_core, y_to_core, diag_to_core):
        copy.wait_recv()
    rows_store = pltpu.make_async_copy(rows, rows_ref, store_sem.at[1])
    rows_store.start()

    far = pick(me, (UP, UP, DOWN, DOWN))
    near = 1 - far

    def pass_on(way, second, hop):
        ag_arrival(way, second, hop - 1).wait_recv()
        ag(way, second, hop).start()

    @pl.when(is_mid)
    def _():
        pass_on(far, 0, 1)
        pass_on(near, 0, 1)

    goal = (
        pick(me, (3, 3, 0, 0)),
        pick(me, (2, 2, 1, 1)),
        pick(me, (1, 0, 3, 2)),
        me,
    )
    way = (far, far, pick(me, (UP, DOWN, UP, DOWN)))
    tile = 256
    tiles = units // tile
    weight_load.wait()

    def compute(index, carry):
        slot = index // tiles
        piece = lax.rem(index, tiles)
        step = slot // 2
        tok = jnp.where(lax.rem(slot, 2) == 0, other_x, gx)
        to = jnp.where(step == 0, goal[0], jnp.where(step == 1, goal[1], jnp.where(step == 2, goal[2], me)))
        here = weight_vmem[pl.ds(pl.multiple_of(to * units + piece * tile, tile), tile), :]
        part[slot, :, pl.ds(pl.multiple_of(piece * tile, tile), tile)] = lax.dot_general(
            rows[tok], here, (((1,), (1,)), ((), ())), preferred_element_type=jnp.float32
        )
        return carry

    def rs(step, second):
        to, where = goal[step], way[step]
        return remote(
            outgoing.at[2 * step + second],
            arrived.at[where, to, second],
            rs_send.at[2 * step + second],
            rs_recv.at[where, to, second],
            {"gz": me + 1 - 2 * where},
        )

    def rs_arrival(where, to, second):
        at = arrived.at[where, to, second]
        return remote(
            at,
            at,
            rs_send.at[2 * 0 + second],
            rs_recv.at[where, to, second],
            {"gz": me - 1 + 2 * where},
        )

    def rs_first(step, second):
        outgoing[2 * step + second] = part[2 * step + second].astype(jnp.bfloat16)
        rs(step, second).start()

    def rs_add(step, second):
        to, where = goal[step], way[step]
        rs_arrival(where, to, second).wait_recv()
        outgoing[2 * step + second] = (
            part[2 * step + second] + arrived[where, to, second].astype(jnp.float32)
        ).astype(jnp.bfloat16)
        rs(step, second).start()

    lax.fori_loop(0, 2 * tiles, compute, 0)

    @pl.when(is_end)
    def _():
        rs_first(0, 0)

    x_hidden_in.wait_recv()
    both_ways(1)
    lax.fori_loop(2 * tiles, 8 * tiles, compute, 0)

    @pl.when(is_end)
    def _():
        ag(far, 0, 0).wait_send()
        rs_first(0, 1)
        rs(0, 0).wait_send()
        rs_first(1, 0)
        ag(far, 1, 0).wait_send()
        rs_first(1, 1)
        rs(0, 1).wait_send()
        rs_first(2, 0)
        rs(1, 0).wait_send()
        rs_first(2, 1)

    @pl.when(is_mid)
    def _():
        rs_add(0, 0)
        pass_on(near, 0, 2)
        pass_on(near, 1, 1)
        pass_on(far, 1, 1)
        rs_add(0, 1)
        rs_add(2, 0)
        rs_add(1, 0)
        pass_on(near, 1, 2)
        rs_add(1, 1)
        rs_add(2, 1)

    def settle(second):
        @pl.when(me > 0)
        def _():
            rs_arrival(UP, me, second).wait_recv()
            part[6 + second] = part[6 + second] + arrived[UP, me, second].astype(jnp.float32)

        @pl.when(me < 3)
        def _():
            rs_arrival(DOWN, me, second).wait_recv()
            part[6 + second] = part[6 + second] + arrived[DOWN, me, second].astype(jnp.float32)

    settle(0)
    outgoing[6] = part[6].astype(jnp.bfloat16)
    x_sum = remote(outgoing.at[6], final.at[gx], x_send.at[1], x_recv.at[1], {"gx": other_x})
    x_sum_in = remote(outgoing.at[6], final.at[other_x], x_send.at[1], x_recv.at[1], {"gx": other_x})
    x_sum.start()
    settle(1)
    final[gx] = part[7].astype(jnp.bfloat16)
    x_sum_in.wait_recv()
    for q in range(cols // group):
        span = slice(q * group, (q + 1) * group)
        pair = jnp.concatenate(
            [final[0, :, q * half : (q + 1) * half], final[1, :, q * half : (q + 1) * half]], axis=1
        )
        total = jnp.dot(pair, select, preferred_element_type=jnp.float32)
        pre_grad_ref[:, span] = (total * slope[:, span]).astype(jnp.bfloat16)

    @pl.when(is_end)
    def _():
        for second in (0, 1):
            for hop in range(3):
                ag_arrival(near, second, hop).wait_recv()
        ag_done = rs(1, 1)
        ag_done.wait_send()
        rs(2, 0).wait_send()
        rs(2, 1).wait_send()

    @pl.when(is_mid)
    def _():
        for second in (0, 1):
            for hop in range(2):
                ag(far, second, hop).wait_send()
            for hop in range(3):
                ag(near, second, hop).wait_send()
            for step in range(3):
                rs(step, second).wait_send()

    for copy in (to_core, to_x, to_y, x_to_y, x_to_core, y_to_core, diag_to_core, x_hidden, x_sum):
        copy.wait_send()
    own_store.wait()
    rows_store.wait()


def exchange(pre_act, grad_out, weight):
    tokens, cols = pre_act.shape
    block, width = grad_out.shape
    units = cols // 2
    bf16, f32 = jnp.bfloat16, jnp.float32
    vmem = pl.BlockSpec(memory_space=pltpu.VMEM)
    anywhere = pl.BlockSpec(memory_space=pl.ANY)
    dma = pltpu.SemaphoreType.DMA
    return pl.pallas_call(
        exchange_kernel,
        out_shape=(
            jax.ShapeDtypeStruct((tokens, cols), bf16),
            jax.ShapeDtypeStruct((2, 4, units, tokens), bf16),
            jax.ShapeDtypeStruct((2, tokens, width), bf16),
        ),
        in_specs=[vmem, vmem, anywhere],
        out_specs=(vmem, anywhere, anywhere),
        scratch_shapes=[
            pltpu.VMEM(weight.shape, bf16),
            pltpu.VMEM((2, tokens, width), bf16),
            pltpu.VMEM((2, units, tokens), bf16),
            pltpu.VMEM((tokens, cols), f32),
            pltpu.VMEM((8, tokens, units), f32),
            pltpu.VMEM((2, 4, 2, tokens, units), bf16),
            pltpu.VMEM((7, tokens, units), bf16),
            pltpu.VMEM((2, tokens, units), bf16),
            dma,
            dma((2,)),
            dma((7,)),
            dma((7,)),
            dma((2,)),
            dma((2,)),
            dma((2, 2, 3)),
            dma((2, 2, 3)),
            dma((6,)),
            dma((2, 4, 2)),
        ],
        compiler_params=pltpu.CompilerParams(
            collective_id=0, has_side_effects=True, vmem_limit_bytes=48 * 1024 * 1024
        ),
        name="exchange",
    )(pre_act, grad_out, weight)


def weight_grad_kernel(hidden_ref, rows_ref, out_ref):
    total = jnp.dot(hidden_ref[0], rows_ref[0], preferred_element_type=jnp.float32)
    total = total + jnp.dot(hidden_ref[1], rows_ref[1], preferred_element_type=jnp.float32)
    out_ref[...] = total.astype(jnp.bfloat16)


def weight_grad_of(hidden, rows):
    _, unit_count, tokens = hidden.shape
    width = rows.shape[2]
    tile = 512
    return pl.pallas_call(
        weight_grad_kernel,
        grid=(unit_count // tile,),
        out_shape=jax.ShapeDtypeStruct((unit_count, width), jnp.bfloat16),
        in_specs=[
            pl.BlockSpec((2, tile, tokens), lambda i: (0, i, 0)),
            pl.BlockSpec((2, tokens, width), lambda i: (0, 0, 0)),
        ],
        out_specs=pl.BlockSpec((tile, width), lambda i: (i, 0)),
        compiler_params=pltpu.CompilerParams(vmem_limit_bytes=32 * 1024 * 1024),
        name="weight_grad",
    )(hidden, rows)


def with_kernel(pre_act, grad_out, weight):
    pre_grad, hidden, rows = exchange(pre_act, grad_out, weight[:, 0, :])
    hidden = hidden.reshape(2, -1, hidden.shape[3])
    return (pre_grad, weight_grad_of(hidden, rows)[:, None, :])


def with_collectives(pre_act, grad_out, weight):
    groups = lax.axis_size("gx")
    tokens, cols = pre_act.shape
    value, slope = gelu_parts(pre_act.astype(jnp.float32))
    split = value.astype(jnp.bfloat16).reshape(tokens, cols // groups, groups).transpose(2, 0, 1)
    hidden = lax.all_to_all(split, "gx", 0, 0, tiled=True)
    hidden = lax.all_gather(hidden, "gz", axis=2, tiled=True)
    hidden = hidden.reshape(groups * tokens, -1)
    grad_rows = lax.all_gather(grad_out, ("gx", "gy"), axis=0, tiled=True)
    partial = jnp.einsum("pd,rd->pr", grad_rows, weight[:, 0, :], preferred_element_type=jnp.float32)
    summed = lax.psum_scatter(partial.astype(jnp.bfloat16), "gz", scatter_dimension=1, tiled=True)
    summed = lax.all_to_all(summed.reshape(groups, tokens, -1), "gx", 0, 0, tiled=True)
    summed = summed.transpose(1, 2, 0).reshape(tokens, cols).astype(jnp.float32)
    pre_grad = (summed * slope).astype(jnp.bfloat16)
    weight_grad = jnp.einsum("pr,pd->rd", hidden, grad_rows, preferred_element_type=jnp.float32)
    return (pre_grad, weight_grad.astype(jnp.bfloat16)[:, None, :])


def solution(mesh):
    sizes = tuple(mesh.shape[name] for name in ("gx", "gy", "gz"))
    placed = (P("gx", ("gy", "gz")), P(("gx", "gy"), "gz"), P("gy", "gx", "gz"))
    return jax.shard_map(
        with_kernel if sizes == (2, 4, 4) else with_collectives,
        mesh=mesh,
        in_specs=placed,
        out_specs=(P("gx", ("gy", "gz")), P("gy", "gx", "gz")),
        check_vma=False,
    )
```

```python
import functools

import jax
import jax.numpy as jnp
from jax import lax
from jax.experimental import pallas as pl
from jax.experimental.pallas import tpu as pltpu
from jax.sharding import PartitionSpec as P

tanh_scale = 0.7978845608028654
cubic_coef = 0.044715
MESH = pl.DeviceIdType.MESH
UP, DOWN = 0, 1


def gelu_parts(inputs):
    inner = tanh_scale * (inputs + cubic_coef * inputs * inputs * inputs)
    tangent = jnp.tanh(inner)
    gelu_value = 0.5 * inputs * (1.0 + tangent)
    gelu_slope = 0.5 * (1.0 + tangent) + 0.5 * inputs * (1.0 - tangent * tangent) * tanh_scale * (
        1.0 + 3.0 * cubic_coef * inputs * inputs
    )
    return (gelu_value, gelu_slope)


def pick(me, values):
    out = jnp.int32(values[0])
    for at in range(1, len(values)):
        out = jnp.where(me == at, jnp.int32(values[at]), out)
    return out


def exchange_kernel(
    pre_ref,
    grad_ref,
    weight_ref,
    pre_grad_ref,
    weight_grad_ref,
    weight_vmem,
    pre_vmem,
    rows,
    hidden,
    other_part,
    slope,
    part,
    arrived,
    outgoing,
    final,
    load_sem,
    grad_send,
    grad_recv,
    x_send,
    x_recv,
    ag_send,
    ag_recv,
    rs_send,
    rs_recv,
):
    gx, gy, me = lax.axis_index("gx"), lax.axis_index("gy"), lax.axis_index("gz")
    other_x = 1 - gx
    core = gy + 1 - 2 * lax.rem(gy, 2)
    far_y = lax.rem(gy + 2, 4)
    is_mid = jnp.logical_and(me > 0, me < 3)
    is_end = jnp.logical_not(is_mid)
    tokens, cols = pre_ref.shape
    block = grad_ref.shape[0]
    width = grad_ref.shape[1]
    units = cols // 2

    barrier = pltpu.get_barrier_semaphore()
    for peer in ({"gy": core}, {"gx": other_x}, {"gy": far_y}):
        pl.semaphore_signal(barrier, inc=1, device_id=peer, device_id_type=MESH)

    @pl.when(me > 0)
    def _():
        pl.semaphore_signal(barrier, inc=1, device_id={"gz": me - 1}, device_id_type=MESH)

    @pl.when(me < 3)
    def _():
        pl.semaphore_signal(barrier, inc=1, device_id={"gz": me + 1}, device_id_type=MESH)

    own_rows = rows.at[gx, pl.ds(pl.multiple_of(gy * block, block), block), :]
    pre_load = pltpu.make_async_copy(pre_ref, pre_vmem, load_sem.at[0])
    pre_load.start()
    grad_load = pltpu.make_async_copy(grad_ref, own_rows, load_sem.at[1])
    grad_load.start()
    weight_load = pltpu.make_async_copy(weight_ref, weight_vmem, load_sem.at[2])
    weight_load.start()
    pl.semaphore_wait(barrier, jnp.where(is_mid, 5, 4))

    def grad_copy(kind, bx, by, peer, src=None):
        at = rows.at[bx, pl.ds(pl.multiple_of(by * block, block), block), :]
        return pltpu.make_async_remote_copy(
            src_ref=at if src is None else src,
            dst_ref=at,
            send_sem=grad_send.at[kind],
            recv_sem=grad_recv.at[kind],
            device_id=peer,
            device_id_type=MESH,
        )

    to_x = grad_copy(1, gx, gy, {"gx": other_x}, grad_ref)
    to_y = grad_copy(2, gx, gy, {"gy": far_y}, grad_ref)
    to_core = grad_copy(0, gx, gy, {"gy": core}, grad_ref)
    to_x.start()
    to_y.start()
    to_core.start()
    pre_load.wait()

    group = 256
    half = group // 2
    line = lax.broadcasted_iota(jnp.int32, (group, group), 0)
    lane = lax.broadcasted_iota(jnp.int32, (group, group), 1)
    target = jnp.where(line < half, 2 * line + gx, 2 * (line - half) + other_x)
    select = jnp.where(lane == target, 1.0, 0.0).astype(jnp.bfloat16)
    for q in range(cols // group):
        span = slice(q * group, (q + 1) * group)
        value, slope_part = gelu_parts(pre_vmem[:, span].astype(jnp.float32))
        slope[:, span] = slope_part
        moved = lax.dot_general(
            select,
            value.astype(jnp.bfloat16),
            (((1,), (1,)), ((), ())),
            preferred_element_type=jnp.float32,
        ).astype(jnp.bfloat16)
        hidden[gx, me, q * half : (q + 1) * half, :] = moved[:half]
        other_part[q * half : (q + 1) * half, :] = moved[half:]

    def remote(src, dst, send, recv, peer):
        return pltpu.make_async_remote_copy(
            src_ref=src,
            dst_ref=dst,
            send_sem=send,
            recv_sem=recv,
            device_id=peer,
            device_id_type=MESH,
        )

    def ag(way, second, hop):
        step = 1 - 2 * way
        owner = me - hop * step
        tok = other_x if second else gx
        at = hidden.at[tok, owner]
        return remote(at, at, ag_send.at[way, second, hop], ag_recv.at[way, second, hop], {"gz": me + step})

    def ag_arrival(way, second, hop):
        step = 1 - 2 * way
        owner = me - step - hop * step
        tok = other_x if second else gx
        at = hidden.at[tok, owner]
        return remote(at, at, ag_send.at[way, second, hop], ag_recv.at[way, second, hop], {"gz": me - step})

    def both_ways(second):
        @pl.when(me < 3)
        def _():
            ag(UP, second, 0).start()

        @pl.when(me > 0)
        def _():
            ag(DOWN, second, 0).start()

    x_hidden = remote(other_part, hidden.at[gx, me], x_send.at[0], x_recv.at[0], {"gx": other_x})
    x_hidden_in = remote(other_part, hidden.at[other_x, me], x_send.at[0], x_recv.at[0], {"gx": other_x})
    x_hidden.start()
    both_ways(0)

    to_x.wait_recv()
    x_to_y = grad_copy(3, other_x, gy, {"gy": far_y})
    x_to_y.start()
    x_to_core = grad_copy(4, other_x, gy, {"gy": core})
    x_to_core.start()
    to_y.wait_recv()
    y_to_core = grad_copy(5, gx, far_y, {"gy": core})
    y_to_core.start()
    x_to_y.wait_recv()
    diag_to_core = grad_copy(6, other_x, far_y, {"gy": core})
    diag_to_core.start()
    for copy in (to_core, x_to_core, y_to_core, diag_to_core):
        copy.wait_recv()
    grad_load.wait()

    far = pick(me, (UP, UP, DOWN, DOWN))
    near = 1 - far

    def pass_on(way, second, hop):
        ag_arrival(way, second, hop - 1).wait_recv()
        ag(way, second, hop).start()

    @pl.when(is_mid)
    def _():
        pass_on(far, 0, 1)
        pass_on(near, 0, 1)

    goal = (
        pick(me, (3, 3, 0, 0)),
        pick(me, (2, 2, 1, 1)),
        pick(me, (1, 0, 3, 2)),
        me,
    )
    way = (far, far, pick(me, (UP, DOWN, UP, DOWN)))
    tile = 256
    tiles = units // tile
    weight_load.wait()

    def compute(index, carry):
        slot = index // tiles
        piece = lax.rem(index, tiles)
        step = slot // 2
        tok = jnp.where(lax.rem(slot, 2) == 0, other_x, gx)
        to = jnp.where(step == 0, goal[0], jnp.where(step == 1, goal[1], jnp.where(step == 2, goal[2], me)))
        here = weight_vmem[pl.ds(pl.multiple_of(to * units + piece * tile, tile), tile), :]
        part[slot, :, pl.ds(pl.multiple_of(piece * tile, tile), tile)] = lax.dot_general(
            rows[tok], here, (((1,), (1,)), ((), ())), preferred_element_type=jnp.float32
        )
        return carry

    def rs(step, second):
        to, where = goal[step], way[step]
        return remote(
            outgoing.at[2 * step + second],
            arrived.at[where, to, second],
            rs_send.at[2 * step + second],
            rs_recv.at[where, to, second],
            {"gz": me + 1 - 2 * where},
        )

    def rs_arrival(where, to, second):
        at = arrived.at[where, to, second]
        return remote(
            at,
            at,
            rs_send.at[2 * 0 + second],
            rs_recv.at[where, to, second],
            {"gz": me - 1 + 2 * where},
        )

    def rs_first(step, second):
        outgoing[2 * step + second] = part[2 * step + second].astype(jnp.bfloat16)
        rs(step, second).start()

    def rs_add(step, second):
        to, where = goal[step], way[step]
        rs_arrival(where, to, second).wait_recv()
        outgoing[2 * step + second] = (
            part[2 * step + second] + arrived[where, to, second].astype(jnp.float32)
        ).astype(jnp.bfloat16)
        rs(step, second).start()

    lax.fori_loop(0, 2 * tiles, compute, 0)

    @pl.when(is_end)
    def _():
        rs_first(0, 0)

    x_hidden_in.wait_recv()
    both_ways(1)
    lax.fori_loop(2 * tiles, 8 * tiles, compute, 0)

    def weight_grad(owner):
        def one(piece, carry):
            at = pl.ds(pl.multiple_of(piece * tile, tile), tile)
            total = jnp.dot(hidden[0, owner, at, :], rows[0], preferred_element_type=jnp.float32)
            total = total + jnp.dot(hidden[1, owner, at, :], rows[1], preferred_element_type=jnp.float32)
            out = pl.ds(pl.multiple_of(owner * units + piece * tile, tile), tile)
            weight_grad_ref[out, :] = total.astype(jnp.bfloat16)
            return carry

        lax.fori_loop(0, tiles, one, 0)

    def arrived_at_end(hop):
        ag_arrival(near, 0, hop).wait_recv()
        ag_arrival(near, 1, hop).wait_recv()

    @pl.when(is_end)
    def _():
        ag(far, 0, 0).wait_send()
        rs_first(0, 1)
        weight_grad(me)
        rs(0, 0).wait_send()
        rs_first(1, 0)
        ag(far, 1, 0).wait_send()
        rs_first(1, 1)
        arrived_at_end(0)
        weight_grad(pick(me, (1, 1, 2, 2)))
        rs(0, 1).wait_send()
        rs_first(2, 0)
        rs(1, 0).wait_send()
        rs_first(2, 1)
        arrived_at_end(1)
        weight_grad(pick(me, (2, 2, 1, 1)))

    @pl.when(is_mid)
    def _():
        rs_add(0, 0)
        weight_grad(me)
        pass_on(near, 0, 2)
        pass_on(near, 1, 1)
        pass_on(far, 1, 1)
        weight_grad(pick(me, (0, 0, 3, 3)))
        rs_add(0, 1)
        weight_grad(3 - me)
        rs_add(2, 0)
        rs_add(1, 0)
        pass_on(near, 1, 2)
        rs_add(1, 1)
        rs_add(2, 1)

    def settle(second):
        @pl.when(me > 0)
        def _():
            rs_arrival(UP, me, second).wait_recv()
            part[6 + second] = part[6 + second] + arrived[UP, me, second].astype(jnp.float32)

        @pl.when(me < 3)
        def _():
            rs_arrival(DOWN, me, second).wait_recv()
            part[6 + second] = part[6 + second] + arrived[DOWN, me, second].astype(jnp.float32)

    settle(0)
    outgoing[6] = part[6].astype(jnp.bfloat16)
    x_sum = remote(outgoing.at[6], final.at[1], x_send.at[1], x_recv.at[1], {"gx": other_x})
    x_sum_in = remote(outgoing.at[6], final.at[1], x_send.at[1], x_recv.at[1], {"gx": other_x})
    x_sum.start()

    @pl.when(is_end)
    def _():
        arrived_at_end(2)

    weight_grad(goal[0])
    settle(1)
    final[0] = part[7].astype(jnp.bfloat16)
    x_sum_in.wait_recv()
    for q in range(cols // group):
        span = slice(q * group, (q + 1) * group)
        pair = jnp.concatenate(
            [final[0, :, q * half : (q + 1) * half], final[1, :, q * half : (q + 1) * half]], axis=1
        )
        total = jnp.dot(pair, select, preferred_element_type=jnp.float32)
        pre_grad_ref[:, span] = (total * slope[:, span]).astype(jnp.bfloat16)

    @pl.when(is_end)
    def _():
        rs(1, 1).wait_send()
        rs(2, 0).wait_send()
        rs(2, 1).wait_send()

    @pl.when(is_mid)
    def _():
        for second in (0, 1):
            for hop in range(2):
                ag(far, second, hop).wait_send()
            for hop in range(3):
                ag(near, second, hop).wait_send()
            for step in range(3):
                rs(step, second).wait_send()

    for copy in (to_core, to_x, to_y, x_to_y, x_to_core, y_to_core, diag_to_core, x_hidden, x_sum):
        copy.wait_send()


def exchange(pre_act, grad_out, weight):
    tokens, cols = pre_act.shape
    block, width = grad_out.shape
    units = cols // 2
    bf16, f32 = jnp.bfloat16, jnp.float32
    vmem = pl.BlockSpec(memory_space=pltpu.VMEM)
    in_hbm = pl.BlockSpec(memory_space=pltpu.HBM)
    dma = pltpu.SemaphoreType.DMA
    return pl.pallas_call(
        exchange_kernel,
        out_shape=(
            pltpu.VMEM((tokens, cols), bf16),
            pltpu.VMEM(weight.shape, bf16),
        ),
        in_specs=[in_hbm, in_hbm, in_hbm],
        out_specs=(vmem, vmem),
        scratch_shapes=[
            pltpu.VMEM(weight.shape, bf16),
            pltpu.VMEM((tokens, cols), bf16),
            pltpu.VMEM((2, tokens, width), bf16),
            pltpu.VMEM((2, 4, units, tokens), bf16),
            pltpu.VMEM((units, tokens), bf16),
            pltpu.VMEM((tokens, cols), f32),
            pltpu.VMEM((8, tokens, units), f32),
            pltpu.VMEM((2, 4, 2, tokens, units), bf16),
            pltpu.VMEM((7, tokens, units), bf16),
            pltpu.VMEM((2, tokens, units), bf16),
            dma((3,)),
            dma((7,)),
            dma((7,)),
            dma((2,)),
            dma((2,)),
            dma((2, 2, 3)),
            dma((2, 2, 3)),
            dma((6,)),
            dma((2, 4, 2)),
        ],
        compiler_params=pltpu.CompilerParams(
            collective_id=0, has_side_effects=True, vmem_limit_bytes=53 * 1024 * 1024
        ),
        name="exchange",
    )(pre_act, grad_out, weight)


def with_kernel(pre_act, grad_out, weight):
    pre_grad, weight_grad = exchange(pre_act, grad_out, weight[:, 0, :])
    return (pre_grad, weight_grad[:, None, :])


def with_collectives(pre_act, grad_out, weight):
    groups = lax.axis_size("gx")
    tokens, cols = pre_act.shape
    value, slope = gelu_parts(pre_act.astype(jnp.float32))
    split = value.astype(jnp.bfloat16).reshape(tokens, cols // groups, groups).transpose(2, 0, 1)
    hidden = lax.all_to_all(split, "gx", 0, 0, tiled=True)
    hidden = lax.all_gather(hidden, "gz", axis=2, tiled=True)
    hidden = hidden.reshape(groups * tokens, -1)
    grad_rows = lax.all_gather(grad_out, ("gx", "gy"), axis=0, tiled=True)
    partial = jnp.einsum("pd,rd->pr", grad_rows, weight[:, 0, :], preferred_element_type=jnp.float32)
    summed = lax.psum_scatter(partial.astype(jnp.bfloat16), "gz", scatter_dimension=1, tiled=True)
    summed = lax.all_to_all(summed.reshape(groups, tokens, -1), "gx", 0, 0, tiled=True)
    summed = summed.transpose(1, 2, 0).reshape(tokens, cols).astype(jnp.float32)
    pre_grad = (summed * slope).astype(jnp.bfloat16)
    weight_grad = jnp.einsum("pr,pd->rd", hidden, grad_rows, preferred_element_type=jnp.float32)
    return (pre_grad, weight_grad.astype(jnp.bfloat16)[:, None, :])


def solution(mesh):
    sizes = tuple(mesh.shape[name] for name in ("gx", "gy", "gz"))
    placed = (P("gx", ("gy", "gz")), P(("gx", "gy"), "gz"), P("gy", "gx", "gz"))
    return jax.shard_map(
        with_kernel if sizes == (2, 4, 4) else with_collectives,
        mesh=mesh,
        in_specs=placed,
        out_specs=(P("gx", ("gy", "gz")), P("gy", "gx", "gz")),
        check_vma=False,
    )
```

```python
import functools

import jax
import jax.numpy as jnp
from jax import lax
from jax.experimental import pallas as pl
from jax.experimental.pallas import tpu as pltpu
from jax.sharding import PartitionSpec as P

tanh_scale = 0.7978845608028654
cubic_coef = 0.044715
MESH = pl.DeviceIdType.MESH
UP, DOWN = 0, 1


def gelu_parts(inputs):
    inner = tanh_scale * (inputs + cubic_coef * inputs * inputs * inputs)
    tangent = jnp.tanh(inner)
    gelu_value = 0.5 * inputs * (1.0 + tangent)
    gelu_slope = 0.5 * (1.0 + tangent) + 0.5 * inputs * (1.0 - tangent * tangent) * tanh_scale * (
        1.0 + 3.0 * cubic_coef * inputs * inputs
    )
    return (gelu_value, gelu_slope)


def pick(me, values):
    out = jnp.int32(values[0])
    for at in range(1, len(values)):
        out = jnp.where(me == at, jnp.int32(values[at]), out)
    return out


def exchange_kernel(
    pre_ref,
    grad_ref,
    weight_ref,
    weight_grad_ref,
    final,
    slope,
    weight_vmem,
    pre_vmem,
    rows,
    hidden,
    other_part,
    part,
    arrived,
    outgoing,
    load_sem,
    grad_send,
    grad_recv,
    x_send,
    x_recv,
    ag_send,
    ag_recv,
    rs_send,
    rs_recv,
):
    gx, gy, me = lax.axis_index("gx"), lax.axis_index("gy"), lax.axis_index("gz")
    other_x = 1 - gx
    core = gy + 1 - 2 * lax.rem(gy, 2)
    far_y = lax.rem(gy + 2, 4)
    is_mid = jnp.logical_and(me > 0, me < 3)
    is_end = jnp.logical_not(is_mid)
    tokens, cols = pre_ref.shape
    block = grad_ref.shape[0]
    width = grad_ref.shape[1]
    units = cols // 2

    barrier = pltpu.get_barrier_semaphore()
    for peer in ({"gy": core}, {"gx": other_x}, {"gy": far_y}):
        pl.semaphore_signal(barrier, inc=1, device_id=peer, device_id_type=MESH)

    @pl.when(me > 0)
    def _():
        pl.semaphore_signal(barrier, inc=1, device_id={"gz": me - 1}, device_id_type=MESH)

    @pl.when(me < 3)
    def _():
        pl.semaphore_signal(barrier, inc=1, device_id={"gz": me + 1}, device_id_type=MESH)

    own_rows = rows.at[gx, pl.ds(pl.multiple_of(gy * block, block), block), :]
    pre_load = pltpu.make_async_copy(pre_ref, pre_vmem, load_sem.at[0])
    pre_load.start()
    grad_load = pltpu.make_async_copy(grad_ref, own_rows, load_sem.at[1])
    grad_load.start()
    weight_load = pltpu.make_async_copy(weight_ref, weight_vmem, load_sem.at[2])
    weight_load.start()

    def grad_copy(kind, bx, by, peer, src=None):
        at = rows.at[bx, pl.ds(pl.multiple_of(by * block, block), block), :]
        return pltpu.make_async_remote_copy(
            src_ref=at if src is None else src,
            dst_ref=at,
            send_sem=grad_send.at[kind],
            recv_sem=grad_recv.at[kind],
            device_id=peer,
            device_id_type=MESH,
        )

    group = 256
    half = group // 2
    line = lax.broadcasted_iota(jnp.int32, (group, group), 0)
    lane = lax.broadcasted_iota(jnp.int32, (group, group), 1)
    target = jnp.where(line < half, 2 * line + gx, 2 * (line - half) + other_x)
    select = jnp.where(lane == target, 1.0, 0.0).astype(jnp.bfloat16)

    def make_hidden(q):
        value = gelu_parts(pre_vmem[:, q * group : (q + 1) * group].astype(jnp.float32))[0]
        moved = lax.dot_general(
            select,
            value.astype(jnp.bfloat16),
            (((1,), (1,)), ((), ())),
            preferred_element_type=jnp.float32,
        ).astype(jnp.bfloat16)
        hidden[gx, me, q * half : (q + 1) * half, :] = moved[:half]
        other_part[q * half : (q + 1) * half, :] = moved[half:]

    groups = cols // group
    pre_load.wait()
    for q in range(groups // 2):
        make_hidden(q)
    pl.semaphore_wait(barrier, jnp.where(is_mid, 5, 4))
    to_x = grad_copy(1, gx, gy, {"gx": other_x}, grad_ref)
    to_y = grad_copy(2, gx, gy, {"gy": far_y}, grad_ref)
    to_core = grad_copy(0, gx, gy, {"gy": core}, grad_ref)
    to_x.start()
    to_y.start()
    to_core.start()

    def remote(src, dst, send, recv, peer):
        return pltpu.make_async_remote_copy(
            src_ref=src,
            dst_ref=dst,
            send_sem=send,
            recv_sem=recv,
            device_id=peer,
            device_id_type=MESH,
        )

    cut = units // 2

    def hidden_piece(owner, piece):
        tok = gx if piece < 2 else other_x
        return hidden.at[tok, owner, pl.ds((piece % 2) * cut, cut), :]

    def ag(way, piece, hop):
        step = 1 - 2 * way
        at = hidden_piece(me - hop * step, piece)
        return remote(at, at, ag_send.at[way, piece, hop], ag_recv.at[way, piece, hop], {"gz": me + step})

    def ag_arrival(way, piece, hop):
        step = 1 - 2 * way
        at = hidden_piece(me - step - hop * step, piece)
        return remote(at, at, ag_send.at[way, piece, hop], ag_recv.at[way, piece, hop], {"gz": me - step})

    def both_ways(piece):
        @pl.when(me < 3)
        def _():
            ag(UP, piece, 0).start()

        @pl.when(me > 0)
        def _():
            ag(DOWN, piece, 0).start()

    def x_hidden(piece, tok):
        span = pl.ds(piece * cut, cut)
        return remote(
            other_part.at[span, :],
            hidden.at[tok, me, span, :],
            x_send.at[piece],
            x_recv.at[piece],
            {"gx": other_x},
        )

    both_ways(0)
    x_hidden(0, gx).start()
    for q in range(groups // 2, groups):
        make_hidden(q)
    both_ways(1)
    x_hidden(1, gx).start()

    to_x.wait_recv()
    x_to_y = grad_copy(3, other_x, gy, {"gy": far_y})
    x_to_y.start()
    x_to_core = grad_copy(4, other_x, gy, {"gy": core})
    x_to_core.start()
    to_y.wait_recv()
    y_to_core = grad_copy(5, gx, far_y, {"gy": core})
    y_to_core.start()
    x_to_y.wait_recv()
    diag_to_core = grad_copy(6, other_x, far_y, {"gy": core})
    diag_to_core.start()
    for copy in (to_core, x_to_core, y_to_core, diag_to_core):
        copy.wait_recv()
    grad_load.wait()

    far = pick(me, (UP, UP, DOWN, DOWN))
    near = 1 - far

    def pass_on(way, piece, hop):
        ag_arrival(way, piece, hop - 1).wait_recv()
        ag(way, piece, hop).start()

    @pl.when(is_mid)
    def _():
        for piece in (0, 1):
            pass_on(far, piece, 1)
            pass_on(near, piece, 1)

    goal = (
        pick(me, (3, 3, 0, 0)),
        pick(me, (2, 2, 1, 1)),
        pick(me, (1, 0, 3, 2)),
        me,
    )
    way = (far, far, pick(me, (UP, DOWN, UP, DOWN)))
    tile = 256
    tiles = units // tile
    weight_load.wait()

    def compute(index, carry):
        slot = index // tiles
        piece = lax.rem(index, tiles)
        step = slot // 2
        tok = jnp.where(lax.rem(slot, 2) == 0, other_x, gx)
        to = jnp.where(step == 0, goal[0], jnp.where(step == 1, goal[1], jnp.where(step == 2, goal[2], me)))
        here = weight_vmem[pl.ds(pl.multiple_of(to * units + piece * tile, tile), tile), :]
        part[slot, :, pl.ds(pl.multiple_of(piece * tile, tile), tile)] = lax.dot_general(
            rows[tok], here, (((1,), (1,)), ((), ())), preferred_element_type=jnp.float32
        )
        return carry

    rows_cut = tokens // 2

    def part_piece(step, piece):
        return part.at[2 * step + piece // 2, pl.ds((piece % 2) * rows_cut, rows_cut), :]

    def rs(step, piece):
        to, where = goal[step], way[step]
        return remote(
            outgoing.at[4 * step + piece],
            arrived.at[where, to, piece],
            rs_send.at[4 * step + piece],
            rs_recv.at[where, to, piece],
            {"gz": me + 1 - 2 * where},
        )

    def rs_arrival(where, to, piece):
        at = arrived.at[where, to, piece]
        return remote(at, at, rs_send.at[piece], rs_recv.at[where, to, piece], {"gz": me - 1 + 2 * where})

    def rs_first(step, second):
        for piece in (2 * second, 2 * second + 1):
            outgoing[4 * step + piece] = part_piece(step, piece)[...].astype(jnp.bfloat16)
            rs(step, piece).start()

    def rs_sent(step, second):
        for piece in (2 * second, 2 * second + 1):
            rs(step, piece).wait_send()

    def rs_add(step, second):
        to, where = goal[step], way[step]
        for piece in (2 * second, 2 * second + 1):
            rs_arrival(where, to, piece).wait_recv()
            outgoing[4 * step + piece] = (
                part_piece(step, piece)[...] + arrived[where, to, piece].astype(jnp.float32)
            ).astype(jnp.bfloat16)
            rs(step, piece).start()

    lax.fori_loop(0, tiles, compute, 0)

    @pl.when(is_end)
    def _():
        rs_first(0, 0)

    for piece in (0, 1):
        x_hidden(piece, other_x).wait_recv()
        both_ways(2 + piece)
    lax.fori_loop(tiles, 8 * tiles, compute, 0)

    def make_slope(q, carry):
        span = pl.ds(pl.multiple_of(q * group, group), group)
        slope[:, span] = gelu_parts(pre_vmem[:, span].astype(jnp.float32))[1]
        return carry

    lax.fori_loop(0, groups, make_slope, 0)

    def weight_grad(owner):
        def one(piece, carry):
            at = pl.ds(pl.multiple_of(piece * tile, tile), tile)
            total = jnp.dot(hidden[0, owner, at, :], rows[0], preferred_element_type=jnp.float32)
            total = total + jnp.dot(hidden[1, owner, at, :], rows[1], preferred_element_type=jnp.float32)
            out = pl.ds(pl.multiple_of(owner * units + piece * tile, tile), tile)
            weight_grad_ref[out, :] = total.astype(jnp.bfloat16)
            return carry

        lax.fori_loop(0, tiles, one, 0)

    def arrived_at_end(hop):
        for piece in range(4):
            ag_arrival(near, piece, hop).wait_recv()

    @pl.when(is_end)
    def _():
        for piece in (0, 1):
            ag(far, piece, 0).wait_send()
        rs_first(0, 1)
        weight_grad(me)
        rs_sent(0, 0)
        rs_first(1, 0)
        for piece in (2, 3):
            ag(far, piece, 0).wait_send()
        rs_first(1, 1)
        arrived_at_end(0)
        weight_grad(pick(me, (1, 1, 2, 2)))
        rs_sent(0, 1)
        rs_first(2, 0)
        rs_sent(1, 0)
        rs_first(2, 1)
        arrived_at_end(1)
        weight_grad(pick(me, (2, 2, 1, 1)))

    @pl.when(is_mid)
    def _():
        rs_add(0, 0)
        weight_grad(me)
        for piece in (0, 1):
            pass_on(near, piece, 2)
        for piece in (2, 3):
            pass_on(near, piece, 1)
            pass_on(far, piece, 1)
        weight_grad(pick(me, (0, 0, 3, 3)))
        rs_add(0, 1)
        weight_grad(3 - me)
        rs_add(2, 0)
        rs_add(1, 0)
        for piece in (2, 3):
            pass_on(near, piece, 2)
        rs_add(1, 1)
        rs_add(2, 1)

    def settle(piece):
        total = part_piece(3, piece)

        @pl.when(me > 0)
        def _():
            rs_arrival(UP, me, piece).wait_recv()
            total[...] = total[...] + arrived[UP, me, piece].astype(jnp.float32)

        @pl.when(me < 3)
        def _():
            rs_arrival(DOWN, me, piece).wait_recv()
            total[...] = total[...] + arrived[DOWN, me, piece].astype(jnp.float32)

        return total[...].astype(jnp.bfloat16)

    def x_sum(piece):
        return remote(
            outgoing.at[12 + piece],
            final.at[1, pl.ds(piece * rows_cut, rows_cut), :],
            x_send.at[2 + piece],
            x_recv.at[2 + piece],
            {"gx": other_x},
        )

    for piece in (0, 1):
        outgoing[12 + piece] = settle(piece)
        x_sum(piece).start()

    @pl.when(is_end)
    def _():
        arrived_at_end(2)

    weight_grad(goal[0])
    for piece in (0, 1):
        final[0, pl.ds(piece * rows_cut, rows_cut), :] = settle(2 + piece)

    @pl.when(is_end)
    def _():
        rs_sent(1, 1)
        rs_sent(2, 0)
        rs_sent(2, 1)

    @pl.when(is_mid)
    def _():
        for piece in range(4):
            for hop in range(2):
                ag(far, piece, hop).wait_send()
            for hop in range(3):
                ag(near, piece, hop).wait_send()
        for step in range(3):
            rs_sent(step, 0)
            rs_sent(step, 1)

    for copy in (to_core, to_x, to_y, x_to_y, x_to_core, y_to_core, diag_to_core):
        copy.wait_send()
    for piece in (0, 1):
        x_hidden(piece, gx).wait_send()
        x_sum(piece).wait_send()
        x_sum(piece).wait_recv()


def exchange(pre_act, grad_out, weight):
    tokens, cols = pre_act.shape
    block, width = grad_out.shape
    units = cols // 2
    bf16, f32 = jnp.bfloat16, jnp.float32
    vmem = pl.BlockSpec(memory_space=pltpu.VMEM)
    in_hbm = pl.BlockSpec(memory_space=pltpu.HBM)
    dma = pltpu.SemaphoreType.DMA
    return pl.pallas_call(
        exchange_kernel,
        out_shape=(
            pltpu.VMEM(weight.shape, bf16),
            pltpu.VMEM((2, tokens, units), bf16),
            pltpu.VMEM((tokens, cols), f32),
        ),
        in_specs=[in_hbm, in_hbm, in_hbm],
        out_specs=(vmem, vmem, vmem),
        scratch_shapes=[
            pltpu.VMEM(weight.shape, bf16),
            pltpu.VMEM((tokens, cols), bf16),
            pltpu.VMEM((2, tokens, width), bf16),
            pltpu.VMEM((2, 4, units, tokens), bf16),
            pltpu.VMEM((units, tokens), bf16),
            pltpu.VMEM((8, tokens, units), f32),
            pltpu.VMEM((2, 4, 4, tokens // 2, units), bf16),
            pltpu.VMEM((14, tokens // 2, units), bf16),
            dma((3,)),
            dma((7,)),
            dma((7,)),
            dma((4,)),
            dma((4,)),
            dma((2, 4, 3)),
            dma((2, 4, 3)),
            dma((12,)),
            dma((2, 4, 4)),
        ],
        compiler_params=pltpu.CompilerParams(
            collective_id=0, has_side_effects=True, vmem_limit_bytes=52 * 1024 * 1024
        ),
        name="exchange",
    )(pre_act, grad_out, weight)


def finish_kernel(weight_grad_ref, sums_ref, slope_ref, pre_grad_out, weight_grad_out, pre_grad, sem):
    own = lax.axis_index("gx")
    copies = []
    count = weight_grad_ref.shape[0] // 4
    for q in range(4):
        span = pl.ds(q * count, count)
        copies.append(
            pltpu.make_async_copy(weight_grad_ref.at[span, :], weight_grad_out.at[span, :], sem.at[q])
        )
        copies[-1].start()
    group = 256
    half = group // 2
    line = lax.broadcasted_iota(jnp.int32, (group, group), 0)
    lane = lax.broadcasted_iota(jnp.int32, (group, group), 1)
    target = jnp.where(line < half, 2 * line + own, 2 * (line - half) + 1 - own)
    select = jnp.where(lane == target, 1.0, 0.0).astype(jnp.bfloat16)
    for q in range(slope_ref.shape[1] // group):
        span = slice(q * group, (q + 1) * group)
        pair = jnp.concatenate(
            [sums_ref[0, :, q * half : (q + 1) * half], sums_ref[1, :, q * half : (q + 1) * half]], axis=1
        )
        total = jnp.dot(pair, select, preferred_element_type=jnp.float32)
        pre_grad[:, span] = (total * slope_ref[:, span]).astype(jnp.bfloat16)
    copies.append(pltpu.make_async_copy(pre_grad, pre_grad_out, sem.at[4]))
    copies[-1].start()
    for copy in copies:
        copy.wait()


def with_kernel(pre_act, grad_out, weight):
    weight_grad, sums, slope = exchange(pre_act, grad_out, weight[:, 0, :])
    vmem = pl.BlockSpec(memory_space=pltpu.VMEM)
    anywhere = pl.BlockSpec(memory_space=pl.ANY)
    pre_grad, weight_grad = pl.pallas_call(
        finish_kernel,
        out_shape=(
            pltpu.HBM(pre_act.shape, jnp.bfloat16),
            pltpu.HBM(weight_grad.shape, jnp.bfloat16),
        ),
        in_specs=[anywhere, vmem, vmem],
        out_specs=(anywhere, anywhere),
        scratch_shapes=[pltpu.VMEM(pre_act.shape, jnp.bfloat16), pltpu.SemaphoreType.DMA((5,))],
        compiler_params=pltpu.CompilerParams(vmem_limit_bytes=8 * 1024 * 1024),
        name="finish",
    )(weight_grad, sums, slope)
    return (pre_grad, weight_grad[:, None, :])


def with_collectives(pre_act, grad_out, weight):
    groups = lax.axis_size("gx")
    tokens, cols = pre_act.shape
    value, slope = gelu_parts(pre_act.astype(jnp.float32))
    split = value.astype(jnp.bfloat16).reshape(tokens, cols // groups, groups).transpose(2, 0, 1)
    hidden = lax.all_to_all(split, "gx", 0, 0, tiled=True)
    hidden = lax.all_gather(hidden, "gz", axis=2, tiled=True)
    hidden = hidden.reshape(groups * tokens, -1)
    grad_rows = lax.all_gather(grad_out, ("gx", "gy"), axis=0, tiled=True)
    partial = jnp.einsum("pd,rd->pr", grad_rows, weight[:, 0, :], preferred_element_type=jnp.float32)
    summed = lax.psum_scatter(partial.astype(jnp.bfloat16), "gz", scatter_dimension=1, tiled=True)
    summed = lax.all_to_all(summed.reshape(groups, tokens, -1), "gx", 0, 0, tiled=True)
    summed = summed.transpose(1, 2, 0).reshape(tokens, cols).astype(jnp.float32)
    pre_grad = (summed * slope).astype(jnp.bfloat16)
    weight_grad = jnp.einsum("pr,pd->rd", hidden, grad_rows, preferred_element_type=jnp.float32)
    return (pre_grad, weight_grad.astype(jnp.bfloat16)[:, None, :])


def solution(mesh):
    sizes = tuple(mesh.shape[name] for name in ("gx", "gy", "gz"))
    placed = (P("gx", ("gy", "gz")), P(("gx", "gy"), "gz"), P("gy", "gx", "gz"))
    return jax.shard_map(
        with_kernel if sizes == (2, 4, 4) else with_collectives,
        mesh=mesh,
        in_specs=placed,
        out_specs=(P("gx", ("gy", "gz")), P("gy", "gx", "gz")),
        check_vma=False,
    )
```

```python
import functools

import jax
import jax.numpy as jnp
from jax import lax
from jax.experimental import pallas as pl
from jax.experimental.pallas import tpu as pltpu
from jax.sharding import PartitionSpec as P

tanh_scale = 0.7978845608028654
cubic_coef = 0.044715
MESH = pl.DeviceIdType.MESH
UP, DOWN = 0, 1


def gelu_parts(inputs):
    inner = tanh_scale * (inputs + cubic_coef * inputs * inputs * inputs)
    tangent = jnp.tanh(inner)
    gelu_value = 0.5 * inputs * (1.0 + tangent)
    gelu_slope = 0.5 * (1.0 + tangent) + 0.5 * inputs * (1.0 - tangent * tangent) * tanh_scale * (
        1.0 + 3.0 * cubic_coef * inputs * inputs
    )
    return (gelu_value, gelu_slope)


def pick(me, values):
    out = jnp.int32(values[0])
    for at in range(1, len(values)):
        out = jnp.where(me == at, jnp.int32(values[at]), out)
    return out


def exchange_kernel(
    pre_ref,
    grad_ref,
    weight_ref,
    weight_grad_ref,
    final,
    slope,
    weight_vmem,
    pre_vmem,
    rows,
    hidden,
    other_part,
    part,
    arrived,
    outgoing,
    load_sem,
    grad_send,
    grad_recv,
    x_send,
    x_recv,
    ag_send,
    ag_recv,
    rs_send,
    rs_recv,
):
    gx, gy, me = lax.axis_index("gx"), lax.axis_index("gy"), lax.axis_index("gz")
    other_x = 1 - gx
    core = gy + 1 - 2 * lax.rem(gy, 2)
    far_y = lax.rem(gy + 2, 4)
    is_mid = jnp.logical_and(me > 0, me < 3)
    is_end = jnp.logical_not(is_mid)
    tokens, cols = pre_ref.shape
    block = grad_ref.shape[0]
    width = grad_ref.shape[1]
    units = cols // 2

    barrier = pltpu.get_barrier_semaphore()
    for peer in ({"gy": core}, {"gx": other_x}, {"gy": far_y}):
        pl.semaphore_signal(barrier, inc=1, device_id=peer, device_id_type=MESH)

    @pl.when(me > 0)
    def _():
        pl.semaphore_signal(barrier, inc=1, device_id={"gz": me - 1}, device_id_type=MESH)

    @pl.when(me < 3)
    def _():
        pl.semaphore_signal(barrier, inc=1, device_id={"gz": me + 1}, device_id_type=MESH)

    own_rows = rows.at[gx, pl.ds(pl.multiple_of(gy * block, block), block), :]
    pre_load = pltpu.make_async_copy(pre_ref, pre_vmem, load_sem.at[0])
    pre_load.start()
    grad_load = pltpu.make_async_copy(grad_ref, own_rows, load_sem.at[1])
    grad_load.start()
    weight_load = pltpu.make_async_copy(weight_ref, weight_vmem, load_sem.at[2])
    weight_load.start()

    def grad_copy(kind, bx, by, peer, src=None):
        at = rows.at[bx, pl.ds(pl.multiple_of(by * block, block), block), :]
        return pltpu.make_async_remote_copy(
            src_ref=at if src is None else src,
            dst_ref=at,
            send_sem=grad_send.at[kind],
            recv_sem=grad_recv.at[kind],
            device_id=peer,
            device_id_type=MESH,
        )

    group = 256
    half = group // 2
    line = lax.broadcasted_iota(jnp.int32, (group, group), 0)
    lane = lax.broadcasted_iota(jnp.int32, (group, group), 1)
    target = jnp.where(line < half, 2 * line + gx, 2 * (line - half) + other_x)
    select = jnp.where(lane == target, 1.0, 0.0).astype(jnp.bfloat16)

    def make_hidden(q):
        value = gelu_parts(pre_vmem[:, q * group : (q + 1) * group].astype(jnp.float32))[0]
        moved = lax.dot_general(
            select,
            value.astype(jnp.bfloat16),
            (((1,), (1,)), ((), ())),
            preferred_element_type=jnp.float32,
        ).astype(jnp.bfloat16)
        hidden[gx, me, q * half : (q + 1) * half, :] = moved[:half]
        other_part[q * half : (q + 1) * half, :] = moved[half:]

    groups = cols // group
    pre_load.wait()
    for q in range(groups // 2):
        make_hidden(q)
    pl.semaphore_wait(barrier, jnp.where(is_mid, 5, 4))
    to_x = grad_copy(1, gx, gy, {"gx": other_x}, grad_ref)
    to_y = grad_copy(2, gx, gy, {"gy": far_y}, grad_ref)
    to_core = grad_copy(0, gx, gy, {"gy": core}, grad_ref)

    def remote(src, dst, send, recv, peer):
        return pltpu.make_async_remote_copy(
            src_ref=src,
            dst_ref=dst,
            send_sem=send,
            recv_sem=recv,
            device_id=peer,
            device_id_type=MESH,
        )

    cut = units // 2

    def hidden_piece(owner, piece):
        tok = gx if piece < 2 else other_x
        return hidden.at[tok, owner, pl.ds((piece % 2) * cut, cut), :]

    def ag(way, piece, hop):
        step = 1 - 2 * way
        at = hidden_piece(me - hop * step, piece)
        return remote(at, at, ag_send.at[way, piece, hop], ag_recv.at[way, piece, hop], {"gz": me + step})

    def ag_arrival(way, piece, hop):
        step = 1 - 2 * way
        at = hidden_piece(me - step - hop * step, piece)
        return remote(at, at, ag_send.at[way, piece, hop], ag_recv.at[way, piece, hop], {"gz": me - step})

    def both_ways(piece):
        @pl.when(me < 3)
        def _():
            ag(UP, piece, 0).start()

        @pl.when(me > 0)
        def _():
            ag(DOWN, piece, 0).start()

    def x_hidden(piece, tok):
        span = pl.ds(piece * cut, cut)
        return remote(
            other_part.at[span, :],
            hidden.at[tok, me, span, :],
            x_send.at[piece],
            x_recv.at[piece],
            {"gx": other_x},
        )

    both_ways(0)
    x_hidden(0, gx).start()
    to_x.start()
    to_y.start()
    to_core.start()
    for q in range(groups // 2, groups):
        make_hidden(q)
    both_ways(1)
    x_hidden(1, gx).start()

    far = pick(me, (UP, UP, DOWN, DOWN))
    near = 1 - far

    def pass_on(way, piece, hop):
        ag_arrival(way, piece, hop - 1).wait_recv()
        ag(way, piece, hop).start()

    def pass_first(piece):
        @pl.when(is_mid)
        def _():
            pass_on(far, piece, 1)
            pass_on(near, piece, 1)

    pass_first(0)
    x_hidden(0, other_x).wait_recv()
    both_ways(2)

    to_x.wait_recv()
    x_to_y = grad_copy(3, other_x, gy, {"gy": far_y})
    x_to_y.start()
    x_to_core = grad_copy(4, other_x, gy, {"gy": core})
    x_to_core.start()
    to_y.wait_recv()
    y_to_core = grad_copy(5, gx, far_y, {"gy": core})
    y_to_core.start()
    pass_first(1)
    x_hidden(1, other_x).wait_recv()
    both_ways(3)
    x_to_y.wait_recv()
    diag_to_core = grad_copy(6, other_x, far_y, {"gy": core})
    diag_to_core.start()
    for copy in (to_core, x_to_core, y_to_core, diag_to_core):
        copy.wait_recv()
    grad_load.wait()

    goal = (
        pick(me, (3, 3, 0, 0)),
        pick(me, (2, 2, 1, 1)),
        pick(me, (1, 0, 3, 2)),
        me,
    )
    way = (far, far, pick(me, (UP, DOWN, UP, DOWN)))
    tile = 256
    tiles = units // tile
    weight_load.wait()

    def compute(index, carry):
        slot = index // tiles
        piece = lax.rem(index, tiles)
        step = slot // 2
        tok = jnp.where(lax.rem(slot, 2) == 0, other_x, gx)
        to = jnp.where(step == 0, goal[0], jnp.where(step == 1, goal[1], jnp.where(step == 2, goal[2], me)))
        here = weight_vmem[pl.ds(pl.multiple_of(to * units + piece * tile, tile), tile), :]
        part[slot, :, pl.ds(pl.multiple_of(piece * tile, tile), tile)] = lax.dot_general(
            rows[tok], here, (((1,), (1,)), ((), ())), preferred_element_type=jnp.float32
        )
        return carry

    rows_cut = tokens // 2

    def part_piece(step, piece):
        return part.at[2 * step + piece // 2, pl.ds((piece % 2) * rows_cut, rows_cut), :]

    def rs(step, piece):
        to, where = goal[step], way[step]
        return remote(
            outgoing.at[4 * step + piece],
            arrived.at[where, to, piece],
            rs_send.at[4 * step + piece],
            rs_recv.at[where, to, piece],
            {"gz": me + 1 - 2 * where},
        )

    def rs_arrival(where, to, piece):
        at = arrived.at[where, to, piece]
        return remote(at, at, rs_send.at[piece], rs_recv.at[where, to, piece], {"gz": me - 1 + 2 * where})

    def rs_first(step, second):
        for piece in (2 * second, 2 * second + 1):
            outgoing[4 * step + piece] = part_piece(step, piece)[...].astype(jnp.bfloat16)
            rs(step, piece).start()

    def rs_sent(step, second):
        for piece in (2 * second, 2 * second + 1):
            rs(step, piece).wait_send()

    def rs_add(step, second):
        to, where = goal[step], way[step]
        for piece in (2 * second, 2 * second + 1):
            rs_arrival(where, to, piece).wait_recv()
            outgoing[4 * step + piece] = (
                part_piece(step, piece)[...] + arrived[where, to, piece].astype(jnp.float32)
            ).astype(jnp.bfloat16)
            rs(step, piece).start()

    lax.fori_loop(0, tiles, compute, 0)

    @pl.when(is_end)
    def _():
        rs_first(0, 0)

    lax.fori_loop(tiles, 8 * tiles, compute, 0)

    def make_slope(q, carry):
        span = pl.ds(pl.multiple_of(q * group, group), group)
        slope[:, span] = gelu_parts(pre_vmem[:, span].astype(jnp.float32))[1]
        return carry

    lax.fori_loop(0, groups, make_slope, 0)

    def weight_grad(owner):
        def one(piece, carry):
            at = pl.ds(pl.multiple_of(piece * tile, tile), tile)
            total = jnp.dot(hidden[0, owner, at, :], rows[0], preferred_element_type=jnp.float32)
            total = total + jnp.dot(hidden[1, owner, at, :], rows[1], preferred_element_type=jnp.float32)
            out = pl.ds(pl.multiple_of(owner * units + piece * tile, tile), tile)
            weight_grad_ref[out, :] = total.astype(jnp.bfloat16)
            return carry

        lax.fori_loop(0, tiles, one, 0)

    def arrived_at_end(hop):
        for piece in range(4):
            ag_arrival(near, piece, hop).wait_recv()

    @pl.when(is_end)
    def _():
        for piece in range(4):
            ag(far, piece, 0).wait_send()
        rs_first(0, 1)
        weight_grad(me)
        rs_sent(0, 0)
        rs_first(1, 0)
        rs_sent(0, 1)
        rs_first(1, 1)
        arrived_at_end(0)
        weight_grad(pick(me, (1, 1, 2, 2)))
        rs_sent(1, 0)
        rs_first(2, 0)
        rs_sent(1, 1)
        rs_first(2, 1)
        arrived_at_end(1)
        weight_grad(pick(me, (2, 2, 1, 1)))

    @pl.when(is_mid)
    def _():
        for piece in (0, 1):
            pass_on(near, piece, 2)
        for piece in (2, 3):
            pass_on(far, piece, 1)
        weight_grad(me)
        for piece in (2, 3):
            pass_on(near, piece, 1)
        rs_add(0, 0)
        weight_grad(pick(me, (0, 0, 3, 3)))
        for piece in (2, 3):
            pass_on(near, piece, 2)
        rs_add(0, 1)
        weight_grad(3 - me)
        rs_add(2, 0)
        rs_add(1, 0)
        rs_add(2, 1)
        rs_add(1, 1)

    def settle(piece):
        total = part_piece(3, piece)

        @pl.when(me > 0)
        def _():
            rs_arrival(UP, me, piece).wait_recv()
            total[...] = total[...] + arrived[UP, me, piece].astype(jnp.float32)

        @pl.when(me < 3)
        def _():
            rs_arrival(DOWN, me, piece).wait_recv()
            total[...] = total[...] + arrived[DOWN, me, piece].astype(jnp.float32)

        return total[...].astype(jnp.bfloat16)

    def x_sum(piece):
        return remote(
            outgoing.at[12 + piece],
            final.at[1, pl.ds(piece * rows_cut, rows_cut), :],
            x_send.at[2 + piece],
            x_recv.at[2 + piece],
            {"gx": other_x},
        )

    for piece in (0, 1):
        outgoing[12 + piece] = settle(piece)
        x_sum(piece).start()

    @pl.when(is_end)
    def _():
        arrived_at_end(2)

    weight_grad(goal[0])
    for piece in (0, 1):
        final[0, pl.ds(piece * rows_cut, rows_cut), :] = settle(2 + piece)

    @pl.when(is_end)
    def _():
        rs_sent(2, 0)
        rs_sent(2, 1)

    @pl.when(is_mid)
    def _():
        for piece in range(4):
            for hop in range(2):
                ag(far, piece, hop).wait_send()
            for hop in range(3):
                ag(near, piece, hop).wait_send()
        for step in range(3):
            rs_sent(step, 0)
            rs_sent(step, 1)

    for copy in (to_core, to_x, to_y, x_to_y, x_to_core, y_to_core, diag_to_core):
        copy.wait_send()
    for piece in (0, 1):
        x_hidden(piece, gx).wait_send()
        x_sum(piece).wait_send()
        x_sum(piece).wait_recv()


def exchange(pre_act, grad_out, weight):
    tokens, cols = pre_act.shape
    block, width = grad_out.shape
    units = cols // 2
    bf16, f32 = jnp.bfloat16, jnp.float32
    vmem = pl.BlockSpec(memory_space=pltpu.VMEM)
    in_hbm = pl.BlockSpec(memory_space=pltpu.HBM)
    dma = pltpu.SemaphoreType.DMA
    return pl.pallas_call(
        exchange_kernel,
        out_shape=(
            pltpu.VMEM(weight.shape, bf16),
            pltpu.VMEM((2, tokens, units), bf16),
            pltpu.VMEM((tokens, cols), f32),
        ),
        in_specs=[in_hbm, in_hbm, in_hbm],
        out_specs=(vmem, vmem, vmem),
        scratch_shapes=[
            pltpu.VMEM(weight.shape, bf16),
            pltpu.VMEM((tokens, cols), bf16),
            pltpu.VMEM((2, tokens, width), bf16),
            pltpu.VMEM((2, 4, units, tokens), bf16),
            pltpu.VMEM((units, tokens), bf16),
            pltpu.VMEM((8, tokens, units), f32),
            pltpu.VMEM((2, 4, 4, tokens // 2, units), bf16),
            pltpu.VMEM((14, tokens // 2, units), bf16),
            dma((3,)),
            dma((7,)),
            dma((7,)),
            dma((4,)),
            dma((4,)),
            dma((2, 4, 3)),
            dma((2, 4, 3)),
            dma((12,)),
            dma((2, 4, 4)),
        ],
        compiler_params=pltpu.CompilerParams(
            collective_id=0, has_side_effects=True, vmem_limit_bytes=52 * 1024 * 1024
        ),
        name="exchange",
    )(pre_act, grad_out, weight)


def finish_kernel(weight_grad_ref, sums_ref, slope_ref, pre_grad_out, weight_grad_out, pre_grad, sem):
    own = lax.axis_index("gx")
    copies = []
    count = weight_grad_ref.shape[0] // 4
    for q in range(4):
        span = pl.ds(q * count, count)
        copies.append(
            pltpu.make_async_copy(weight_grad_ref.at[span, :], weight_grad_out.at[span, :], sem.at[q])
        )
        copies[-1].start()
    group = 256
    half = group // 2
    line = lax.broadcasted_iota(jnp.int32, (group, group), 0)
    lane = lax.broadcasted_iota(jnp.int32, (group, group), 1)
    target = jnp.where(line < half, 2 * line + own, 2 * (line - half) + 1 - own)
    select = jnp.where(lane == target, 1.0, 0.0).astype(jnp.bfloat16)
    for q in range(slope_ref.shape[1] // group):
        span = slice(q * group, (q + 1) * group)
        pair = jnp.concatenate(
            [sums_ref[0, :, q * half : (q + 1) * half], sums_ref[1, :, q * half : (q + 1) * half]], axis=1
        )
        total = jnp.dot(pair, select, preferred_element_type=jnp.float32)
        pre_grad[:, span] = (total * slope_ref[:, span]).astype(jnp.bfloat16)
    copies.append(pltpu.make_async_copy(pre_grad, pre_grad_out, sem.at[4]))
    copies[-1].start()
    for copy in copies:
        copy.wait()


def with_kernel(pre_act, grad_out, weight):
    weight_grad, sums, slope = exchange(pre_act, grad_out, weight[:, 0, :])
    vmem = pl.BlockSpec(memory_space=pltpu.VMEM)
    anywhere = pl.BlockSpec(memory_space=pl.ANY)
    pre_grad, weight_grad = pl.pallas_call(
        finish_kernel,
        out_shape=(
            pltpu.HBM(pre_act.shape, jnp.bfloat16),
            pltpu.HBM(weight_grad.shape, jnp.bfloat16),
        ),
        in_specs=[anywhere, vmem, vmem],
        out_specs=(anywhere, anywhere),
        scratch_shapes=[pltpu.VMEM(pre_act.shape, jnp.bfloat16), pltpu.SemaphoreType.DMA((5,))],
        compiler_params=pltpu.CompilerParams(vmem_limit_bytes=8 * 1024 * 1024),
        name="finish",
    )(weight_grad, sums, slope)
    return (pre_grad, weight_grad[:, None, :])


def with_collectives(pre_act, grad_out, weight):
    groups = lax.axis_size("gx")
    tokens, cols = pre_act.shape
    value, slope = gelu_parts(pre_act.astype(jnp.float32))
    split = value.astype(jnp.bfloat16).reshape(tokens, cols // groups, groups).transpose(2, 0, 1)
    hidden = lax.all_to_all(split, "gx", 0, 0, tiled=True)
    hidden = lax.all_gather(hidden, "gz", axis=2, tiled=True)
    hidden = hidden.reshape(groups * tokens, -1)
    grad_rows = lax.all_gather(grad_out, ("gx", "gy"), axis=0, tiled=True)
    partial = jnp.einsum("pd,rd->pr", grad_rows, weight[:, 0, :], preferred_element_type=jnp.float32)
    summed = lax.psum_scatter(partial.astype(jnp.bfloat16), "gz", scatter_dimension=1, tiled=True)
    summed = lax.all_to_all(summed.reshape(groups, tokens, -1), "gx", 0, 0, tiled=True)
    summed = summed.transpose(1, 2, 0).reshape(tokens, cols).astype(jnp.float32)
    pre_grad = (summed * slope).astype(jnp.bfloat16)
    weight_grad = jnp.einsum("pr,pd->rd", hidden, grad_rows, preferred_element_type=jnp.float32)
    return (pre_grad, weight_grad.astype(jnp.bfloat16)[:, None, :])


def solution(mesh):
    sizes = tuple(mesh.shape[name] for name in ("gx", "gy", "gz"))
    placed = (P("gx", ("gy", "gz")), P(("gx", "gy"), "gz"), P("gy", "gx", "gz"))
    return jax.shard_map(
        with_kernel if sizes == (2, 4, 4) else with_collectives,
        mesh=mesh,
        in_specs=placed,
        out_specs=(P("gx", ("gy", "gz")), P("gy", "gx", "gz")),
        check_vma=False,
    )
```

```python
import functools

import jax
import jax.numpy as jnp
from jax import lax
from jax.experimental import pallas as pl
from jax.experimental.pallas import tpu as pltpu
from jax.sharding import PartitionSpec as P

tanh_scale = 0.7978845608028654
cubic_coef = 0.044715
MESH = pl.DeviceIdType.MESH
UP, DOWN = 0, 1


def gelu_parts(inputs):
    inner = tanh_scale * (inputs + cubic_coef * inputs * inputs * inputs)
    tangent = jnp.tanh(inner)
    gelu_value = 0.5 * inputs * (1.0 + tangent)
    gelu_slope = 0.5 * (1.0 + tangent) + 0.5 * inputs * (1.0 - tangent * tangent) * tanh_scale * (
        1.0 + 3.0 * cubic_coef * inputs * inputs
    )
    return (gelu_value, gelu_slope)


def pick(me, values):
    out = jnp.int32(values[0])
    for at in range(1, len(values)):
        out = jnp.where(me == at, jnp.int32(values[at]), out)
    return out


def exchange_kernel(
    pre_ref,
    grad_ref,
    weight_ref,
    weight_grad_ref,
    final,
    slope,
    weight_vmem,
    pre_vmem,
    rows,
    hidden,
    other_part,
    part,
    arrived,
    outgoing,
    load_sem,
    grad_send,
    grad_recv,
    x_send,
    x_recv,
    ag_send,
    ag_recv,
    rs_send,
    rs_recv,
):
    gx, gy, me = lax.axis_index("gx"), lax.axis_index("gy"), lax.axis_index("gz")
    other_x = 1 - gx
    core = gy + 1 - 2 * lax.rem(gy, 2)
    far_y = lax.rem(gy + 2, 4)
    is_mid = jnp.logical_and(me > 0, me < 3)
    is_end = jnp.logical_not(is_mid)
    tokens, cols = pre_ref.shape
    block = grad_ref.shape[0]
    width = grad_ref.shape[1]
    units = cols // 2

    barrier = pltpu.get_barrier_semaphore()
    for peer in ({"gy": core}, {"gx": other_x}, {"gy": far_y}):
        pl.semaphore_signal(barrier, inc=1, device_id=peer, device_id_type=MESH)

    @pl.when(me > 0)
    def _():
        pl.semaphore_signal(barrier, inc=1, device_id={"gz": me - 1}, device_id_type=MESH)

    @pl.when(me < 3)
    def _():
        pl.semaphore_signal(barrier, inc=1, device_id={"gz": me + 1}, device_id_type=MESH)

    own_rows = rows.at[gx, pl.ds(pl.multiple_of(gy * block, block), block), :]
    pre_load = pltpu.make_async_copy(pre_ref, pre_vmem, load_sem.at[0])
    pre_load.start()
    grad_load = pltpu.make_async_copy(grad_ref, own_rows, load_sem.at[1])
    grad_load.start()
    weight_load = pltpu.make_async_copy(weight_ref, weight_vmem, load_sem.at[2])
    weight_load.start()

    def grad_copy(kind, bx, by, peer, src=None):
        at = rows.at[bx, pl.ds(pl.multiple_of(by * block, block), block), :]
        return pltpu.make_async_remote_copy(
            src_ref=at if src is None else src,
            dst_ref=at,
            send_sem=grad_send.at[kind],
            recv_sem=grad_recv.at[kind],
            device_id=peer,
            device_id_type=MESH,
        )

    group = 256
    half = group // 2
    line = lax.broadcasted_iota(jnp.int32, (group, group), 0)
    lane = lax.broadcasted_iota(jnp.int32, (group, group), 1)
    target = jnp.where(line < half, 2 * line + gx, 2 * (line - half) + other_x)
    select = jnp.where(lane == target, 1.0, 0.0).astype(jnp.bfloat16)

    def make_hidden(q):
        value = gelu_parts(pre_vmem[:, q * group : (q + 1) * group].astype(jnp.float32))[0]
        moved = lax.dot_general(
            select,
            value.astype(jnp.bfloat16),
            (((1,), (1,)), ((), ())),
            preferred_element_type=jnp.float32,
        ).astype(jnp.bfloat16)
        hidden[gx, me, q * half : (q + 1) * half, :] = moved[:half]
        other_part[q * half : (q + 1) * half, :] = moved[half:]

    groups = cols // group
    pre_load.wait()
    for q in range(groups // 2):
        make_hidden(q)
    pl.semaphore_wait(barrier, jnp.where(is_mid, 5, 4))
    to_x = grad_copy(1, gx, gy, {"gx": other_x}, grad_ref)
    to_y = grad_copy(2, gx, gy, {"gy": far_y}, grad_ref)
    to_core = grad_copy(0, gx, gy, {"gy": core}, grad_ref)

    def remote(src, dst, send, recv, peer):
        return pltpu.make_async_remote_copy(
            src_ref=src,
            dst_ref=dst,
            send_sem=send,
            recv_sem=recv,
            device_id=peer,
            device_id_type=MESH,
        )

    cut = units // 2

    def hidden_piece(owner, piece):
        tok = gx if piece < 2 else other_x
        return hidden.at[tok, owner, pl.ds((piece % 2) * cut, cut), :]

    def ag(way, piece, hop):
        step = 1 - 2 * way
        at = hidden_piece(me - hop * step, piece)
        return remote(at, at, ag_send.at[way, piece, hop], ag_recv.at[way, piece, hop], {"gz": me + step})

    def ag_arrival(way, piece, hop):
        step = 1 - 2 * way
        at = hidden_piece(me - step - hop * step, piece)
        return remote(at, at, ag_send.at[way, piece, hop], ag_recv.at[way, piece, hop], {"gz": me - step})

    def both_ways(piece):
        @pl.when(me < 3)
        def _():
            ag(UP, piece, 0).start()

        @pl.when(me > 0)
        def _():
            ag(DOWN, piece, 0).start()

    def x_hidden(piece, tok):
        span = pl.ds(piece * cut, cut)
        return remote(
            other_part.at[span, :],
            hidden.at[tok, me, span, :],
            x_send.at[piece],
            x_recv.at[piece],
            {"gx": other_x},
        )

    both_ways(0)
    x_hidden(0, gx).start()
    to_y.start()
    to_core.start()
    for q in range(groups // 2, groups):
        make_hidden(q)
    both_ways(1)
    x_hidden(1, gx).start()
    to_x.start()

    far = pick(me, (UP, UP, DOWN, DOWN))
    near = 1 - far

    def pass_on(way, piece, hop):
        ag_arrival(way, piece, hop - 1).wait_recv()
        ag(way, piece, hop).start()

    def pass_first(piece):
        @pl.when(is_mid)
        def _():
            pass_on(far, piece, 1)
            pass_on(near, piece, 1)

    pass_first(0)
    x_hidden(0, other_x).wait_recv()
    both_ways(2)

    to_y.wait_recv()
    y_to_core = grad_copy(5, gx, far_y, {"gy": core})
    y_to_core.start()
    pass_first(1)
    x_hidden(1, other_x).wait_recv()
    both_ways(3)
    to_core.wait_recv()
    y_to_core.wait_recv()
    grad_load.wait()

    goal = (
        pick(me, (3, 3, 0, 0)),
        pick(me, (2, 2, 1, 1)),
        pick(me, (1, 0, 3, 2)),
        me,
    )
    way = (far, far, pick(me, (UP, DOWN, UP, DOWN)))
    tile = 256
    tiles = units // tile
    weight_load.wait()

    def compute(index, carry):
        order = index // tiles
        slot = jnp.where(order < 2, 1 - order, order)
        piece = lax.rem(index, tiles)
        step = slot // 2
        tok = jnp.where(lax.rem(slot, 2) == 0, other_x, gx)
        to = jnp.where(step == 0, goal[0], jnp.where(step == 1, goal[1], jnp.where(step == 2, goal[2], me)))
        here = weight_vmem[pl.ds(pl.multiple_of(to * units + piece * tile, tile), tile), :]
        part[slot, :, pl.ds(pl.multiple_of(piece * tile, tile), tile)] = lax.dot_general(
            rows[tok], here, (((1,), (1,)), ((), ())), preferred_element_type=jnp.float32
        )
        return carry

    rows_cut = tokens // 2

    def part_piece(step, piece):
        return part.at[2 * step + piece // 2, pl.ds((piece % 2) * rows_cut, rows_cut), :]

    def rs(step, piece):
        to, where = goal[step], way[step]
        return remote(
            outgoing.at[4 * step + piece],
            arrived.at[where, to, piece],
            rs_send.at[4 * step + piece],
            rs_recv.at[where, to, piece],
            {"gz": me + 1 - 2 * where},
        )

    def rs_arrival(where, to, piece):
        at = arrived.at[where, to, piece]
        return remote(at, at, rs_send.at[piece], rs_recv.at[where, to, piece], {"gz": me - 1 + 2 * where})

    def rs_first(step, second):
        for piece in (2 * second, 2 * second + 1):
            outgoing[4 * step + piece] = part_piece(step, piece)[...].astype(jnp.bfloat16)
            rs(step, piece).start()

    def rs_sent(step, second):
        for piece in (2 * second, 2 * second + 1):
            rs(step, piece).wait_send()

    def rs_add(step, second):
        to, where = goal[step], way[step]
        for piece in (2 * second, 2 * second + 1):
            rs_arrival(where, to, piece).wait_recv()
            outgoing[4 * step + piece] = (
                part_piece(step, piece)[...] + arrived[where, to, piece].astype(jnp.float32)
            ).astype(jnp.bfloat16)
            rs(step, piece).start()

    lax.fori_loop(0, tiles, compute, 0)

    @pl.when(is_end)
    def _():
        rs_first(0, 1)

    to_x.wait_recv()
    x_to_y = grad_copy(3, other_x, gy, {"gy": far_y})
    x_to_y.start()
    x_to_core = grad_copy(4, other_x, gy, {"gy": core})
    x_to_core.start()

    @pl.when(is_mid)
    def _():
        for piece in (0, 1):
            pass_on(near, piece, 2)

    x_to_y.wait_recv()
    diag_to_core = grad_copy(6, other_x, far_y, {"gy": core})
    diag_to_core.start()
    x_to_core.wait_recv()
    diag_to_core.wait_recv()
    lax.fori_loop(tiles, 8 * tiles, compute, 0)

    def make_slope(q, carry):
        span = pl.ds(pl.multiple_of(q * group, group), group)
        slope[:, span] = gelu_parts(pre_vmem[:, span].astype(jnp.float32))[1]
        return carry

    lax.fori_loop(0, groups, make_slope, 0)

    def weight_grad(owner):
        def one(piece, carry):
            at = pl.ds(pl.multiple_of(piece * tile, tile), tile)
            total = jnp.dot(hidden[0, owner, at, :], rows[0], preferred_element_type=jnp.float32)
            total = total + jnp.dot(hidden[1, owner, at, :], rows[1], preferred_element_type=jnp.float32)
            out = pl.ds(pl.multiple_of(owner * units + piece * tile, tile), tile)
            weight_grad_ref[out, :] = total.astype(jnp.bfloat16)
            return carry

        lax.fori_loop(0, tiles, one, 0)

    def arrived_at_end(hop):
        for piece in range(4):
            ag_arrival(near, piece, hop).wait_recv()

    @pl.when(is_end)
    def _():
        for piece in range(4):
            ag(far, piece, 0).wait_send()
        rs_first(0, 0)
        weight_grad(me)
        rs_sent(0, 1)
        rs_first(1, 0)
        rs_sent(0, 0)
        rs_first(1, 1)
        arrived_at_end(0)
        weight_grad(pick(me, (1, 1, 2, 2)))
        rs_sent(1, 0)
        rs_first(2, 0)
        rs_sent(1, 1)
        rs_first(2, 1)
        arrived_at_end(1)
        weight_grad(pick(me, (2, 2, 1, 1)))

    @pl.when(is_mid)
    def _():
        for piece in (2, 3):
            pass_on(far, piece, 1)
        weight_grad(me)
        for piece in (2, 3):
            pass_on(near, piece, 1)
        rs_add(0, 1)
        weight_grad(pick(me, (0, 0, 3, 3)))
        for piece in (2, 3):
            pass_on(near, piece, 2)
        rs_add(0, 0)
        weight_grad(3 - me)
        rs_add(2, 0)
        rs_add(1, 0)
        rs_add(2, 1)
        rs_add(1, 1)

    def settle(piece):
        total = part_piece(3, piece)

        @pl.when(me > 0)
        def _():
            rs_arrival(UP, me, piece).wait_recv()
            total[...] = total[...] + arrived[UP, me, piece].astype(jnp.float32)

        @pl.when(me < 3)
        def _():
            rs_arrival(DOWN, me, piece).wait_recv()
            total[...] = total[...] + arrived[DOWN, me, piece].astype(jnp.float32)

        return total[...].astype(jnp.bfloat16)

    def x_sum(piece):
        return remote(
            outgoing.at[12 + piece],
            final.at[1, pl.ds(piece * rows_cut, rows_cut), :],
            x_send.at[2 + piece],
            x_recv.at[2 + piece],
            {"gx": other_x},
        )

    for piece in (0, 1):
        outgoing[12 + piece] = settle(piece)
        x_sum(piece).start()

    @pl.when(is_end)
    def _():
        arrived_at_end(2)

    weight_grad(goal[0])
    for piece in (0, 1):
        final[0, pl.ds(piece * rows_cut, rows_cut), :] = settle(2 + piece)

    @pl.when(is_end)
    def _():
        rs_sent(2, 0)
        rs_sent(2, 1)

    @pl.when(is_mid)
    def _():
        for piece in range(4):
            for hop in range(2):
                ag(far, piece, hop).wait_send()
            for hop in range(3):
                ag(near, piece, hop).wait_send()
        for step in range(3):
            rs_sent(step, 0)
            rs_sent(step, 1)

    for copy in (to_core, to_x, to_y, x_to_y, x_to_core, y_to_core, diag_to_core):
        copy.wait_send()
    for piece in (0, 1):
        x_hidden(piece, gx).wait_send()
        x_sum(piece).wait_send()
        x_sum(piece).wait_recv()


def exchange(pre_act, grad_out, weight):
    tokens, cols = pre_act.shape
    block, width = grad_out.shape
    units = cols // 2
    bf16, f32 = jnp.bfloat16, jnp.float32
    vmem = pl.BlockSpec(memory_space=pltpu.VMEM)
    in_hbm = pl.BlockSpec(memory_space=pltpu.HBM)
    dma = pltpu.SemaphoreType.DMA
    return pl.pallas_call(
        exchange_kernel,
        out_shape=(
            pltpu.VMEM(weight.shape, bf16),
            pltpu.VMEM((2, tokens, units), bf16),
            pltpu.VMEM((tokens, cols), f32),
        ),
        in_specs=[in_hbm, in_hbm, in_hbm],
        out_specs=(vmem, vmem, vmem),
        scratch_shapes=[
            pltpu.VMEM(weight.shape, bf16),
            pltpu.VMEM((tokens, cols), bf16),
            pltpu.VMEM((2, tokens, width), bf16),
            pltpu.VMEM((2, 4, units, tokens), bf16),
            pltpu.VMEM((units, tokens), bf16),
            pltpu.VMEM((8, tokens, units), f32),
            pltpu.VMEM((2, 4, 4, tokens // 2, units), bf16),
            pltpu.VMEM((14, tokens // 2, units), bf16),
            dma((3,)),
            dma((7,)),
            dma((7,)),
            dma((4,)),
            dma((4,)),
            dma((2, 4, 3)),
            dma((2, 4, 3)),
            dma((12,)),
            dma((2, 4, 4)),
        ],
        compiler_params=pltpu.CompilerParams(
            collective_id=0, has_side_effects=True, vmem_limit_bytes=52 * 1024 * 1024
        ),
        name="exchange",
    )(pre_act, grad_out, weight)


def finish_kernel(weight_grad_ref, sums_ref, slope_ref, pre_grad_out, weight_grad_out, pre_grad, sem):
    own = lax.axis_index("gx")
    copies = []
    count = weight_grad_ref.shape[0] // 4
    for q in range(4):
        span = pl.ds(q * count, count)
        copies.append(
            pltpu.make_async_copy(weight_grad_ref.at[span, :], weight_grad_out.at[span, :], sem.at[q])
        )
        copies[-1].start()
    group = 256
    half = group // 2
    line = lax.broadcasted_iota(jnp.int32, (group, group), 0)
    lane = lax.broadcasted_iota(jnp.int32, (group, group), 1)
    target = jnp.where(line < half, 2 * line + own, 2 * (line - half) + 1 - own)
    select = jnp.where(lane == target, 1.0, 0.0).astype(jnp.bfloat16)
    for q in range(slope_ref.shape[1] // group):
        span = slice(q * group, (q + 1) * group)
        pair = jnp.concatenate(
            [sums_ref[0, :, q * half : (q + 1) * half], sums_ref[1, :, q * half : (q + 1) * half]], axis=1
        )
        total = jnp.dot(pair, select, preferred_element_type=jnp.float32)
        pre_grad[:, span] = (total * slope_ref[:, span]).astype(jnp.bfloat16)
        copies.append(
            pltpu.make_async_copy(pre_grad.at[:, span], pre_grad_out.at[:, span], sem.at[4 + q])
        )
        copies[-1].start()
    for copy in copies:
        copy.wait()


def with_kernel(pre_act, grad_out, weight):
    weight_grad, sums, slope = exchange(pre_act, grad_out, weight[:, 0, :])
    vmem = pl.BlockSpec(memory_space=pltpu.VMEM)
    anywhere = pl.BlockSpec(memory_space=pl.ANY)
    pre_grad, weight_grad = pl.pallas_call(
        finish_kernel,
        out_shape=(
            pltpu.HBM(pre_act.shape, jnp.bfloat16),
            pltpu.HBM(weight_grad.shape, jnp.bfloat16),
        ),
        in_specs=[anywhere, vmem, vmem],
        out_specs=(anywhere, anywhere),
        scratch_shapes=[pltpu.VMEM(pre_act.shape, jnp.bfloat16), pltpu.SemaphoreType.DMA((4 + pre_act.shape[1] // 256,))],
        compiler_params=pltpu.CompilerParams(vmem_limit_bytes=8 * 1024 * 1024),
        name="finish",
    )(weight_grad, sums, slope)
    return (pre_grad, weight_grad[:, None, :])


def with_collectives(pre_act, grad_out, weight):
    groups = lax.axis_size("gx")
    tokens, cols = pre_act.shape
    value, slope = gelu_parts(pre_act.astype(jnp.float32))
    split = value.astype(jnp.bfloat16).reshape(tokens, cols // groups, groups).transpose(2, 0, 1)
    hidden = lax.all_to_all(split, "gx", 0, 0, tiled=True)
    hidden = lax.all_gather(hidden, "gz", axis=2, tiled=True)
    hidden = hidden.reshape(groups * tokens, -1)
    grad_rows = lax.all_gather(grad_out, ("gx", "gy"), axis=0, tiled=True)
    partial = jnp.einsum("pd,rd->pr", grad_rows, weight[:, 0, :], preferred_element_type=jnp.float32)
    summed = lax.psum_scatter(partial.astype(jnp.bfloat16), "gz", scatter_dimension=1, tiled=True)
    summed = lax.all_to_all(summed.reshape(groups, tokens, -1), "gx", 0, 0, tiled=True)
    summed = summed.transpose(1, 2, 0).reshape(tokens, cols).astype(jnp.float32)
    pre_grad = (summed * slope).astype(jnp.bfloat16)
    weight_grad = jnp.einsum("pr,pd->rd", hidden, grad_rows, preferred_element_type=jnp.float32)
    return (pre_grad, weight_grad.astype(jnp.bfloat16)[:, None, :])


def solution(mesh):
    sizes = tuple(mesh.shape[name] for name in ("gx", "gy", "gz"))
    placed = (P("gx", ("gy", "gz")), P(("gx", "gy"), "gz"), P("gy", "gx", "gz"))
    return jax.shard_map(
        with_kernel if sizes == (2, 4, 4) else with_collectives,
        mesh=mesh,
        in_specs=placed,
        out_specs=(P("gx", ("gy", "gz")), P("gy", "gx", "gz")),
        check_vma=False,
    )
```

```python
import functools

import jax
import jax.numpy as jnp
from jax import lax
from jax.experimental import pallas as pl
from jax.experimental.pallas import tpu as pltpu
from jax.sharding import PartitionSpec as P

tanh_scale = 0.7978845608028654
cubic_coef = 0.044715
MESH = pl.DeviceIdType.MESH
UP, DOWN = 0, 1


def gelu_parts(inputs):
    inner = tanh_scale * (inputs + cubic_coef * inputs * inputs * inputs)
    tangent = jnp.tanh(inner)
    gelu_value = 0.5 * inputs * (1.0 + tangent)
    gelu_slope = 0.5 * (1.0 + tangent) + 0.5 * inputs * (1.0 - tangent * tangent) * tanh_scale * (
        1.0 + 3.0 * cubic_coef * inputs * inputs
    )
    return (gelu_value, gelu_slope)


def pick(me, values):
    out = jnp.int32(values[0])
    for at in range(1, len(values)):
        out = jnp.where(me == at, jnp.int32(values[at]), out)
    return out


def exchange_kernel(
    pre_ref,
    grad_ref,
    weight_ref,
    weight_grad_ref,
    final,
    slope,
    weight_vmem,
    pre_vmem,
    rows,
    hidden,
    other_part,
    part,
    arrived,
    outgoing,
    load_sem,
    grad_send,
    grad_recv,
    x_send,
    x_recv,
    ag_send,
    ag_recv,
    rs_send,
    rs_recv,
):
    gx, gy, me = lax.axis_index("gx"), lax.axis_index("gy"), lax.axis_index("gz")
    other_x = 1 - gx
    core = gy + 1 - 2 * lax.rem(gy, 2)
    far_y = lax.rem(gy + 2, 4)
    is_mid = jnp.logical_and(me > 0, me < 3)
    is_end = jnp.logical_not(is_mid)
    tokens, cols = pre_ref.shape
    block = grad_ref.shape[0]
    width = grad_ref.shape[1]
    units = cols // 2

    barrier = pltpu.get_barrier_semaphore()
    for peer in ({"gy": core}, {"gx": other_x}, {"gy": far_y}):
        pl.semaphore_signal(barrier, inc=1, device_id=peer, device_id_type=MESH)

    @pl.when(me > 0)
    def _():
        pl.semaphore_signal(barrier, inc=1, device_id={"gz": me - 1}, device_id_type=MESH)

    @pl.when(me < 3)
    def _():
        pl.semaphore_signal(barrier, inc=1, device_id={"gz": me + 1}, device_id_type=MESH)

    own_rows = rows.at[gx, pl.ds(pl.multiple_of(gy * block, block), block), :]
    pre_load = pltpu.make_async_copy(pre_ref, pre_vmem, load_sem.at[0])
    pre_load.start()
    grad_load = pltpu.make_async_copy(grad_ref, own_rows, load_sem.at[1])
    grad_load.start()
    weight_load = pltpu.make_async_copy(weight_ref, weight_vmem, load_sem.at[2])
    weight_load.start()

    def grad_copy(kind, bx, by, peer, src=None):
        at = rows.at[bx, pl.ds(pl.multiple_of(by * block, block), block), :]
        return pltpu.make_async_remote_copy(
            src_ref=at if src is None else src,
            dst_ref=at,
            send_sem=grad_send.at[kind],
            recv_sem=grad_recv.at[kind],
            device_id=peer,
            device_id_type=MESH,
        )

    group = 256
    half = group // 2
    line = lax.broadcasted_iota(jnp.int32, (group, group), 0)
    lane = lax.broadcasted_iota(jnp.int32, (group, group), 1)
    target = jnp.where(line < half, 2 * line + gx, 2 * (line - half) + other_x)
    select = jnp.where(lane == target, 1.0, 0.0).astype(jnp.bfloat16)

    def make_hidden(q):
        value = gelu_parts(pre_vmem[:, q * group : (q + 1) * group].astype(jnp.float32))[0]
        moved = lax.dot_general(
            select,
            value.astype(jnp.bfloat16),
            (((1,), (1,)), ((), ())),
            preferred_element_type=jnp.float32,
        ).astype(jnp.bfloat16)
        hidden[gx, me, q * half : (q + 1) * half, :] = moved[:half]
        other_part[q * half : (q + 1) * half, :] = moved[half:]

    groups = cols // group
    pre_load.wait()
    for q in range(groups // 2):
        make_hidden(q)
    pl.semaphore_wait(barrier, jnp.where(is_mid, 5, 4))
    to_x = grad_copy(1, gx, gy, {"gx": other_x}, grad_ref)
    to_y = grad_copy(2, gx, gy, {"gy": far_y}, grad_ref)
    to_core = grad_copy(0, gx, gy, {"gy": core}, grad_ref)

    def remote(src, dst, send, recv, peer):
        return pltpu.make_async_remote_copy(
            src_ref=src,
            dst_ref=dst,
            send_sem=send,
            recv_sem=recv,
            device_id=peer,
            device_id_type=MESH,
        )

    cut = units // 2

    def hidden_piece(owner, piece):
        tok = gx if piece < 2 else other_x
        return hidden.at[tok, owner, pl.ds((piece % 2) * cut, cut), :]

    def ag(way, piece, hop):
        step = 1 - 2 * way
        at = hidden_piece(me - hop * step, piece)
        return remote(at, at, ag_send.at[way, piece, hop], ag_recv.at[way, piece, hop], {"gz": me + step})

    def ag_arrival(way, piece, hop):
        step = 1 - 2 * way
        at = hidden_piece(me - step - hop * step, piece)
        return remote(at, at, ag_send.at[way, piece, hop], ag_recv.at[way, piece, hop], {"gz": me - step})

    def both_ways(piece):
        @pl.when(me < 3)
        def _():
            ag(UP, piece, 0).start()

        @pl.when(me > 0)
        def _():
            ag(DOWN, piece, 0).start()

    def x_hidden(piece, tok):
        span = pl.ds(piece * cut, cut)
        return remote(
            other_part.at[span, :],
            hidden.at[tok, me, span, :],
            x_send.at[piece],
            x_recv.at[piece],
            {"gx": other_x},
        )

    both_ways(0)
    x_hidden(0, gx).start()
    to_y.start()
    to_core.start()
    for q in range(groups // 2, groups):
        make_hidden(q)
    both_ways(1)
    x_hidden(1, gx).start()
    to_x.start()

    far = pick(me, (UP, UP, DOWN, DOWN))
    near = 1 - far

    def pass_on(way, piece, hop):
        ag_arrival(way, piece, hop - 1).wait_recv()
        ag(way, piece, hop).start()

    def pass_first(piece):
        @pl.when(is_mid)
        def _():
            pass_on(far, piece, 1)
            pass_on(near, piece, 1)

    pass_first(0)
    x_hidden(0, other_x).wait_recv()
    both_ways(2)

    to_y.wait_recv()
    y_to_core = grad_copy(5, gx, far_y, {"gy": core})
    y_to_core.start()
    pass_first(1)
    x_hidden(1, other_x).wait_recv()
    both_ways(3)
    to_core.wait_recv()
    y_to_core.wait_recv()
    grad_load.wait()

    goal = (
        pick(me, (3, 3, 0, 0)),
        pick(me, (2, 2, 1, 1)),
        pick(me, (1, 0, 3, 2)),
        me,
    )
    way = (far, far, pick(me, (UP, DOWN, UP, DOWN)))
    tile = 256
    tiles = units // tile
    weight_load.wait()

    def compute(index, carry):
        order = index // tiles
        slot = jnp.where(order < 2, 1 - order, order)
        piece = lax.rem(index, tiles)
        step = slot // 2
        tok = jnp.where(lax.rem(slot, 2) == 0, other_x, gx)
        to = jnp.where(step == 0, goal[0], jnp.where(step == 1, goal[1], jnp.where(step == 2, goal[2], me)))
        here = weight_vmem[pl.ds(pl.multiple_of(to * units + piece * tile, tile), tile), :]
        part[slot, :, pl.ds(pl.multiple_of(piece * tile, tile), tile)] = lax.dot_general(
            rows[tok], here, (((1,), (1,)), ((), ())), preferred_element_type=jnp.float32
        )
        return carry

    rows_cut = tokens // 2

    def part_piece(step, piece):
        return part.at[2 * step + piece // 2, pl.ds((piece % 2) * rows_cut, rows_cut), :]

    def rs(step, piece):
        to, where = goal[step], way[step]
        return remote(
            outgoing.at[4 * step + piece],
            arrived.at[where, to, piece],
            rs_send.at[4 * step + piece],
            rs_recv.at[where, to, piece],
            {"gz": me + 1 - 2 * where},
        )

    def rs_arrival(where, to, piece):
        at = arrived.at[where, to, piece]
        return remote(at, at, rs_send.at[piece], rs_recv.at[where, to, piece], {"gz": me - 1 + 2 * where})

    def rs_first(step, second):
        for piece in (2 * second, 2 * second + 1):
            outgoing[4 * step + piece] = part_piece(step, piece)[...].astype(jnp.bfloat16)
            rs(step, piece).start()

    def rs_sent(step, second):
        for piece in (2 * second, 2 * second + 1):
            rs(step, piece).wait_send()

    def rs_add(step, second):
        to, where = goal[step], way[step]
        for piece in (2 * second, 2 * second + 1):
            rs_arrival(where, to, piece).wait_recv()
            outgoing[4 * step + piece] = (
                part_piece(step, piece)[...] + arrived[where, to, piece].astype(jnp.float32)
            ).astype(jnp.bfloat16)
            rs(step, piece).start()

    lax.fori_loop(0, tiles, compute, 0)

    @pl.when(is_end)
    def _():
        rs_first(0, 1)

    to_x.wait_recv()
    x_to_y = grad_copy(3, other_x, gy, {"gy": far_y})
    x_to_y.start()
    x_to_core = grad_copy(4, other_x, gy, {"gy": core})
    x_to_core.start()

    x_to_y.wait_recv()
    diag_to_core = grad_copy(6, other_x, far_y, {"gy": core})
    diag_to_core.start()
    x_to_core.wait_recv()
    diag_to_core.wait_recv()
    lax.fori_loop(tiles, 2 * tiles, compute, 0)

    @pl.when(is_end)
    def _():
        rs_first(0, 0)

    @pl.when(is_mid)
    def _():
        for piece in (0, 1):
            pass_on(near, piece, 2)
        for piece in (2, 3):
            pass_on(far, piece, 1)
            pass_on(near, piece, 1)
        rs_add(0, 1)

    lax.fori_loop(2 * tiles, 8 * tiles, compute, 0)

    def make_slope(q, carry):
        span = pl.ds(pl.multiple_of(q * group, group), group)
        slope[:, span] = gelu_parts(pre_vmem[:, span].astype(jnp.float32))[1]
        return carry

    lax.fori_loop(0, groups, make_slope, 0)

    def weight_grad(owner):
        def one(piece, carry):
            at = pl.ds(pl.multiple_of(piece * tile, tile), tile)
            total = jnp.dot(hidden[0, owner, at, :], rows[0], preferred_element_type=jnp.float32)
            total = total + jnp.dot(hidden[1, owner, at, :], rows[1], preferred_element_type=jnp.float32)
            out = pl.ds(pl.multiple_of(owner * units + piece * tile, tile), tile)
            weight_grad_ref[out, :] = total.astype(jnp.bfloat16)
            return carry

        lax.fori_loop(0, tiles, one, 0)

    def arrived_at_end(hop):
        for piece in range(4):
            ag_arrival(near, piece, hop).wait_recv()

    @pl.when(is_end)
    def _():
        for piece in range(4):
            ag(far, piece, 0).wait_send()
        weight_grad(me)
        rs_sent(0, 1)
        rs_first(1, 0)
        rs_sent(0, 0)
        rs_first(1, 1)
        arrived_at_end(0)
        weight_grad(pick(me, (1, 1, 2, 2)))
        rs_sent(1, 0)
        rs_first(2, 0)
        rs_sent(1, 1)
        rs_first(2, 1)
        arrived_at_end(1)
        weight_grad(pick(me, (2, 2, 1, 1)))

    @pl.when(is_mid)
    def _():
        weight_grad(me)
        weight_grad(pick(me, (0, 0, 3, 3)))
        for piece in (2, 3):
            pass_on(near, piece, 2)
        rs_add(0, 0)
        weight_grad(3 - me)
        rs_add(2, 0)
        rs_add(1, 0)
        rs_add(2, 1)
        rs_add(1, 1)

    def settle(piece):
        total = part_piece(3, piece)

        @pl.when(me > 0)
        def _():
            rs_arrival(UP, me, piece).wait_recv()
            total[...] = total[...] + arrived[UP, me, piece].astype(jnp.float32)

        @pl.when(me < 3)
        def _():
            rs_arrival(DOWN, me, piece).wait_recv()
            total[...] = total[...] + arrived[DOWN, me, piece].astype(jnp.float32)

        return total[...].astype(jnp.bfloat16)

    def x_sum(piece):
        return remote(
            outgoing.at[12 + piece],
            final.at[1, pl.ds(piece * rows_cut, rows_cut), :],
            x_send.at[2 + piece],
            x_recv.at[2 + piece],
            {"gx": other_x},
        )

    for piece in (0, 1):
        outgoing[12 + piece] = settle(piece)
        x_sum(piece).start()

    @pl.when(is_end)
    def _():
        arrived_at_end(2)

    weight_grad(goal[0])
    for piece in (0, 1):
        final[0, pl.ds(piece * rows_cut, rows_cut), :] = settle(2 + piece)

    @pl.when(is_end)
    def _():
        rs_sent(2, 0)
        rs_sent(2, 1)

    @pl.when(is_mid)
    def _():
        for piece in range(4):
            for hop in range(2):
                ag(far, piece, hop).wait_send()
            for hop in range(3):
                ag(near, piece, hop).wait_send()
        for step in range(3):
            rs_sent(step, 0)
            rs_sent(step, 1)

    for copy in (to_core, to_x, to_y, x_to_y, x_to_core, y_to_core, diag_to_core):
        copy.wait_send()
    for piece in (0, 1):
        x_hidden(piece, gx).wait_send()
        x_sum(piece).wait_send()
        x_sum(piece).wait_recv()


def exchange(pre_act, grad_out, weight):
    tokens, cols = pre_act.shape
    block, width = grad_out.shape
    units = cols // 2
    bf16, f32 = jnp.bfloat16, jnp.float32
    vmem = pl.BlockSpec(memory_space=pltpu.VMEM)
    in_hbm = pl.BlockSpec(memory_space=pltpu.HBM)
    dma = pltpu.SemaphoreType.DMA
    return pl.pallas_call(
        exchange_kernel,
        out_shape=(
            pltpu.VMEM(weight.shape, bf16),
            pltpu.VMEM((2, tokens, units), bf16),
            pltpu.VMEM((tokens, cols), f32),
        ),
        in_specs=[in_hbm, in_hbm, in_hbm],
        out_specs=(vmem, vmem, vmem),
        scratch_shapes=[
            pltpu.VMEM(weight.shape, bf16),
            pltpu.VMEM((tokens, cols), bf16),
            pltpu.VMEM((2, tokens, width), bf16),
            pltpu.VMEM((2, 4, units, tokens), bf16),
            pltpu.VMEM((units, tokens), bf16),
            pltpu.VMEM((8, tokens, units), f32),
            pltpu.VMEM((2, 4, 4, tokens // 2, units), bf16),
            pltpu.VMEM((14, tokens // 2, units), bf16),
            dma((3,)),
            dma((7,)),
            dma((7,)),
            dma((4,)),
            dma((4,)),
            dma((2, 4, 3)),
            dma((2, 4, 3)),
            dma((12,)),
            dma((2, 4, 4)),
        ],
        compiler_params=pltpu.CompilerParams(
            collective_id=0, has_side_effects=True, vmem_limit_bytes=52 * 1024 * 1024
        ),
        name="exchange",
    )(pre_act, grad_out, weight)


def finish_kernel(weight_grad_ref, sums_ref, slope_ref, pre_grad_out, weight_grad_out, pre_grad, sem):
    own = lax.axis_index("gx")
    copies = []
    count = weight_grad_ref.shape[0] // 4
    for q in range(4):
        span = pl.ds(q * count, count)
        copies.append(
            pltpu.make_async_copy(weight_grad_ref.at[span, :], weight_grad_out.at[span, :], sem.at[q])
        )
        copies[-1].start()
    group = 256
    half = group // 2
    line = lax.broadcasted_iota(jnp.int32, (group, group), 0)
    lane = lax.broadcasted_iota(jnp.int32, (group, group), 1)
    target = jnp.where(line < half, 2 * line + own, 2 * (line - half) + 1 - own)
    select = jnp.where(lane == target, 1.0, 0.0).astype(jnp.bfloat16)
    for q in range(slope_ref.shape[1] // group):
        span = slice(q * group, (q + 1) * group)
        pair = jnp.concatenate(
            [sums_ref[0, :, q * half : (q + 1) * half], sums_ref[1, :, q * half : (q + 1) * half]], axis=1
        )
        total = jnp.dot(pair, select, preferred_element_type=jnp.float32)
        pre_grad[:, span] = (total * slope_ref[:, span]).astype(jnp.bfloat16)
        copies.append(
            pltpu.make_async_copy(pre_grad.at[:, span], pre_grad_out.at[:, span], sem.at[4 + q])
        )
        copies[-1].start()
    for copy in copies:
        copy.wait()


def with_kernel(pre_act, grad_out, weight):
    weight_grad, sums, slope = exchange(pre_act, grad_out, weight[:, 0, :])
    vmem = pl.BlockSpec(memory_space=pltpu.VMEM)
    anywhere = pl.BlockSpec(memory_space=pl.ANY)
    pre_grad, weight_grad = pl.pallas_call(
        finish_kernel,
        out_shape=(
            pltpu.HBM(pre_act.shape, jnp.bfloat16),
            pltpu.HBM(weight_grad.shape, jnp.bfloat16),
        ),
        in_specs=[anywhere, vmem, vmem],
        out_specs=(anywhere, anywhere),
        scratch_shapes=[pltpu.VMEM(pre_act.shape, jnp.bfloat16), pltpu.SemaphoreType.DMA((4 + pre_act.shape[1] // 256,))],
        compiler_params=pltpu.CompilerParams(vmem_limit_bytes=8 * 1024 * 1024),
        name="finish",
    )(weight_grad, sums, slope)
    return (pre_grad, weight_grad[:, None, :])


def with_collectives(pre_act, grad_out, weight):
    groups = lax.axis_size("gx")
    tokens, cols = pre_act.shape
    value, slope = gelu_parts(pre_act.astype(jnp.float32))
    split = value.astype(jnp.bfloat16).reshape(tokens, cols // groups, groups).transpose(2, 0, 1)
    hidden = lax.all_to_all(split, "gx", 0, 0, tiled=True)
    hidden = lax.all_gather(hidden, "gz", axis=2, tiled=True)
    hidden = hidden.reshape(groups * tokens, -1)
    grad_rows = lax.all_gather(grad_out, ("gx", "gy"), axis=0, tiled=True)
    partial = jnp.einsum("pd,rd->pr", grad_rows, weight[:, 0, :], preferred_element_type=jnp.float32)
    summed = lax.psum_scatter(partial.astype(jnp.bfloat16), "gz", scatter_dimension=1, tiled=True)
    summed = lax.all_to_all(summed.reshape(groups, tokens, -1), "gx", 0, 0, tiled=True)
    summed = summed.transpose(1, 2, 0).reshape(tokens, cols).astype(jnp.float32)
    pre_grad = (summed * slope).astype(jnp.bfloat16)
    weight_grad = jnp.einsum("pr,pd->rd", hidden, grad_rows, preferred_element_type=jnp.float32)
    return (pre_grad, weight_grad.astype(jnp.bfloat16)[:, None, :])


def solution(mesh):
    sizes = tuple(mesh.shape[name] for name in ("gx", "gy", "gz"))
    placed = (P("gx", ("gy", "gz")), P(("gx", "gy"), "gz"), P("gy", "gx", "gz"))
    return jax.shard_map(
        with_kernel if sizes == (2, 4, 4) else with_collectives,
        mesh=mesh,
        in_specs=placed,
        out_specs=(P("gx", ("gy", "gz")), P("gy", "gx", "gz")),
        check_vma=False,
    )
```

```python
import functools

import jax
import jax.numpy as jnp
from jax import lax
from jax.experimental import pallas as pl
from jax.experimental.pallas import tpu as pltpu
from jax.sharding import PartitionSpec as P

tanh_scale = 0.7978845608028654
cubic_coef = 0.044715
MESH = pl.DeviceIdType.MESH
UP, DOWN = 0, 1


def gelu_parts(inputs):
    inner = tanh_scale * (inputs + cubic_coef * inputs * inputs * inputs)
    tangent = jnp.tanh(inner)
    gelu_value = 0.5 * inputs * (1.0 + tangent)
    gelu_slope = 0.5 * (1.0 + tangent) + 0.5 * inputs * (1.0 - tangent * tangent) * tanh_scale * (
        1.0 + 3.0 * cubic_coef * inputs * inputs
    )
    return (gelu_value, gelu_slope)


def pick(me, values):
    out = jnp.int32(values[0])
    for at in range(1, len(values)):
        out = jnp.where(me == at, jnp.int32(values[at]), out)
    return out


def exchange_kernel(
    pre_ref,
    grad_ref,
    weight_ref,
    weight_grad_ref,
    final,
    slope,
    weight_vmem,
    pre_vmem,
    rows,
    hidden,
    other_part,
    part,
    arrived,
    outgoing,
    load_sem,
    grad_send,
    grad_recv,
    x_send,
    x_recv,
    ag_send,
    ag_recv,
    rs_send,
    rs_recv,
):
    gx, gy, me = lax.axis_index("gx"), lax.axis_index("gy"), lax.axis_index("gz")
    other_x = 1 - gx
    core = gy + 1 - 2 * lax.rem(gy, 2)
    far_y = lax.rem(gy + 2, 4)
    is_mid = jnp.logical_and(me > 0, me < 3)
    is_end = jnp.logical_not(is_mid)
    tokens, cols = pre_ref.shape
    block = grad_ref.shape[0]
    width = grad_ref.shape[1]
    units = cols // 2

    barrier = pltpu.get_barrier_semaphore()
    for peer in ({"gy": core}, {"gx": other_x}, {"gy": far_y}):
        pl.semaphore_signal(barrier, inc=1, device_id=peer, device_id_type=MESH)

    @pl.when(me > 0)
    def _():
        pl.semaphore_signal(barrier, inc=1, device_id={"gz": me - 1}, device_id_type=MESH)

    @pl.when(me < 3)
    def _():
        pl.semaphore_signal(barrier, inc=1, device_id={"gz": me + 1}, device_id_type=MESH)

    own_rows = rows.at[gx, pl.ds(pl.multiple_of(gy * block, block), block), :]
    pre_load = pltpu.make_async_copy(pre_ref, pre_vmem, load_sem.at[0])
    pre_load.start()
    grad_load = pltpu.make_async_copy(grad_ref, own_rows, load_sem.at[1])
    grad_load.start()
    weight_load = pltpu.make_async_copy(weight_ref, weight_vmem, load_sem.at[2])
    weight_load.start()

    def grad_copy(kind, bx, by, peer, src=None):
        at = rows.at[bx, pl.ds(pl.multiple_of(by * block, block), block), :]
        return pltpu.make_async_remote_copy(
            src_ref=at if src is None else src,
            dst_ref=at,
            send_sem=grad_send.at[kind],
            recv_sem=grad_recv.at[kind],
            device_id=peer,
            device_id_type=MESH,
        )

    group = 256
    half = group // 2
    line = lax.broadcasted_iota(jnp.int32, (group, group), 0)
    lane = lax.broadcasted_iota(jnp.int32, (group, group), 1)
    target = jnp.where(line < half, 2 * line + gx, 2 * (line - half) + other_x)
    select = jnp.where(lane == target, 1.0, 0.0).astype(jnp.bfloat16)

    def make_hidden(q):
        value = gelu_parts(pre_vmem[:, q * group : (q + 1) * group].astype(jnp.float32))[0]
        moved = lax.dot_general(
            select,
            value.astype(jnp.bfloat16),
            (((1,), (1,)), ((), ())),
            preferred_element_type=jnp.float32,
        ).astype(jnp.bfloat16)
        hidden[gx, me, q * half : (q + 1) * half, :] = moved[:half]
        other_part[q * half : (q + 1) * half, :] = moved[half:]

    groups = cols // group
    pre_load.wait()
    for q in range(groups // 2):
        make_hidden(q)
    pl.semaphore_wait(barrier, jnp.where(is_mid, 5, 4))
    to_x = grad_copy(1, gx, gy, {"gx": other_x}, grad_ref)
    to_y = grad_copy(2, gx, gy, {"gy": far_y}, grad_ref)
    to_core = grad_copy(0, gx, gy, {"gy": core}, grad_ref)

    def remote(src, dst, send, recv, peer):
        return pltpu.make_async_remote_copy(
            src_ref=src,
            dst_ref=dst,
            send_sem=send,
            recv_sem=recv,
            device_id=peer,
            device_id_type=MESH,
        )

    cut = units // 2

    def hidden_piece(owner, piece):
        tok = gx if piece < 2 else other_x
        return hidden.at[tok, owner, pl.ds((piece % 2) * cut, cut), :]

    def ag(way, piece, hop):
        step = 1 - 2 * way
        at = hidden_piece(me - hop * step, piece)
        return remote(at, at, ag_send.at[way, piece, hop], ag_recv.at[way, piece, hop], {"gz": me + step})

    def ag_arrival(way, piece, hop):
        step = 1 - 2 * way
        at = hidden_piece(me - step - hop * step, piece)
        return remote(at, at, ag_send.at[way, piece, hop], ag_recv.at[way, piece, hop], {"gz": me - step})

    def both_ways(piece):
        @pl.when(me < 3)
        def _():
            ag(UP, piece, 0).start()

        @pl.when(me > 0)
        def _():
            ag(DOWN, piece, 0).start()

    def x_hidden(piece, tok):
        span = pl.ds(piece * cut, cut)
        return remote(
            other_part.at[span, :],
            hidden.at[tok, me, span, :],
            x_send.at[piece],
            x_recv.at[piece],
            {"gx": other_x},
        )

    both_ways(0)
    x_hidden(0, gx).start()
    to_y.start()
    to_core.start()
    for q in range(groups // 2, groups):
        make_hidden(q)
    both_ways(1)
    x_hidden(1, gx).start()
    to_x.start()

    far = pick(me, (UP, UP, DOWN, DOWN))
    near = 1 - far

    def pass_on(way, piece, hop):
        ag_arrival(way, piece, hop - 1).wait_recv()
        ag(way, piece, hop).start()

    def pass_first(piece):
        @pl.when(is_mid)
        def _():
            pass_on(far, piece, 1)
            pass_on(near, piece, 1)

    pass_first(0)
    x_hidden(0, other_x).wait_recv()
    both_ways(2)

    to_y.wait_recv()
    y_to_core = grad_copy(5, gx, far_y, {"gy": core})
    y_to_core.start()
    pass_first(1)
    x_hidden(1, other_x).wait_recv()
    both_ways(3)
    to_core.wait_recv()
    y_to_core.wait_recv()
    grad_load.wait()

    goal = (
        pick(me, (3, 3, 0, 0)),
        pick(me, (2, 2, 1, 1)),
        pick(me, (1, 0, 3, 2)),
        me,
    )
    way = (far, far, pick(me, (UP, DOWN, UP, DOWN)))
    tile = 256
    tiles = units // tile
    weight_load.wait()

    def compute(index, carry):
        order = index // tiles
        slot = jnp.where(order < 2, 1 - order, order)
        piece = lax.rem(index, tiles)
        step = slot // 2
        tok = jnp.where(lax.rem(slot, 2) == 0, other_x, gx)
        to = jnp.where(step == 0, goal[0], jnp.where(step == 1, goal[1], jnp.where(step == 2, goal[2], me)))
        here = weight_vmem[pl.ds(pl.multiple_of(to * units + piece * tile, tile), tile), :]
        part[slot, :, pl.ds(pl.multiple_of(piece * tile, tile), tile)] = lax.dot_general(
            rows[tok], here, (((1,), (1,)), ((), ())), preferred_element_type=jnp.float32
        )
        return carry

    rows_cut = tokens // 2

    def part_piece(step, piece):
        return part.at[2 * step + piece // 2, pl.ds((piece % 2) * rows_cut, rows_cut), :]

    def rs(step, piece):
        to, where = goal[step], way[step]
        return remote(
            outgoing.at[4 * step + piece],
            arrived.at[where, to, piece],
            rs_send.at[4 * step + piece],
            rs_recv.at[where, to, piece],
            {"gz": me + 1 - 2 * where},
        )

    def rs_arrival(where, to, piece):
        at = arrived.at[where, to, piece]
        return remote(at, at, rs_send.at[piece], rs_recv.at[where, to, piece], {"gz": me - 1 + 2 * where})

    def rs_first(step, second):
        for piece in (2 * second, 2 * second + 1):
            outgoing[4 * step + piece] = part_piece(step, piece)[...].astype(jnp.bfloat16)
            rs(step, piece).start()

    def rs_sent(step, second):
        for piece in (2 * second, 2 * second + 1):
            rs(step, piece).wait_send()

    def rs_add(step, second):
        to, where = goal[step], way[step]
        for piece in (2 * second, 2 * second + 1):
            rs_arrival(where, to, piece).wait_recv()
            outgoing[4 * step + piece] = (
                part_piece(step, piece)[...] + arrived[where, to, piece].astype(jnp.float32)
            ).astype(jnp.bfloat16)
            rs(step, piece).start()

    lax.fori_loop(0, tiles, compute, 0)

    @pl.when(is_end)
    def _():
        rs_first(0, 1)

    to_x.wait_recv()
    x_to_y = grad_copy(3, other_x, gy, {"gy": far_y})
    x_to_y.start()
    x_to_core = grad_copy(4, other_x, gy, {"gy": core})
    x_to_core.start()

    x_to_y.wait_recv()
    diag_to_core = grad_copy(6, other_x, far_y, {"gy": core})
    diag_to_core.start()
    x_to_core.wait_recv()
    diag_to_core.wait_recv()
    lax.fori_loop(tiles, 2 * tiles, compute, 0)

    @pl.when(is_end)
    def _():
        rs_first(0, 0)

    @pl.when(is_mid)
    def _():
        for piece in (0, 1):
            pass_on(near, piece, 2)
        for piece in (2, 3):
            pass_on(far, piece, 1)
            pass_on(near, piece, 1)
        rs_add(0, 1)

    lax.fori_loop(2 * tiles, 8 * tiles, compute, 0)

    def make_slope(q, carry):
        span = pl.ds(pl.multiple_of(q * group, group), group)
        slope[:, span] = gelu_parts(pre_vmem[:, span].astype(jnp.float32))[1]
        return carry

    lax.fori_loop(0, groups, make_slope, 0)

    def weight_grad(owner):
        def one(piece, carry):
            at = pl.ds(pl.multiple_of(piece * tile, tile), tile)
            total = jnp.dot(hidden[0, owner, at, :], rows[0], preferred_element_type=jnp.float32)
            total = total + jnp.dot(hidden[1, owner, at, :], rows[1], preferred_element_type=jnp.float32)
            out = pl.ds(pl.multiple_of(owner * units + piece * tile, tile), tile)
            weight_grad_ref[out, :] = total.astype(jnp.bfloat16)
            return carry

        lax.fori_loop(0, tiles, one, 0)

    def arrived_at_end(hop):
        for piece in range(4):
            ag_arrival(near, piece, hop).wait_recv()

    @pl.when(is_end)
    def _():
        for piece in range(4):
            ag(far, piece, 0).wait_send()
        weight_grad(me)
        rs_sent(0, 1)
        rs_first(1, 0)
        rs_sent(0, 0)
        rs_first(1, 1)
        arrived_at_end(0)
        weight_grad(pick(me, (1, 1, 2, 2)))
        rs_sent(1, 0)
        rs_first(2, 0)
        rs_sent(1, 1)
        arrived_at_end(1)
        weight_grad(pick(me, (2, 2, 1, 1)))
        rs_sent(2, 0)
        rs_first(2, 1)

    @pl.when(is_mid)
    def _():
        weight_grad(me)
        weight_grad(pick(me, (0, 0, 3, 3)))
        for piece in (2, 3):
            pass_on(near, piece, 2)
        rs_add(0, 0)
        weight_grad(3 - me)
        rs_add(2, 0)
        rs_add(1, 0)
        rs_sent(2, 0)
        rs_add(2, 1)
        rs_sent(1, 0)
        rs_add(1, 1)

    def settle(piece):
        total = part_piece(3, piece)

        @pl.when(me > 0)
        def _():
            rs_arrival(UP, me, piece).wait_recv()
            total[...] = total[...] + arrived[UP, me, piece].astype(jnp.float32)

        @pl.when(me < 3)
        def _():
            rs_arrival(DOWN, me, piece).wait_recv()
            total[...] = total[...] + arrived[DOWN, me, piece].astype(jnp.float32)

        return total[...].astype(jnp.bfloat16)

    def x_sum(piece):
        return remote(
            outgoing.at[12 + piece],
            final.at[1, pl.ds(piece * rows_cut, rows_cut), :],
            x_send.at[2 + piece],
            x_recv.at[2 + piece],
            {"gx": other_x},
        )

    for piece in (0, 1):
        outgoing[12 + piece] = settle(piece)
        x_sum(piece).start()

    @pl.when(is_end)
    def _():
        arrived_at_end(2)

    weight_grad(goal[0])
    for piece in (0, 1):
        final[0, pl.ds(piece * rows_cut, rows_cut), :] = settle(2 + piece)

    @pl.when(is_end)
    def _():
        rs_sent(2, 1)

    @pl.when(is_mid)
    def _():
        for piece in range(4):
            for hop in range(2):
                ag(far, piece, hop).wait_send()
            for hop in range(3):
                ag(near, piece, hop).wait_send()
        rs_sent(0, 0)
        for step in range(3):
            rs_sent(step, 1)

    for copy in (to_core, to_x, to_y, x_to_y, x_to_core, y_to_core, diag_to_core):
        copy.wait_send()
    for piece in (0, 1):
        x_hidden(piece, gx).wait_send()
        x_sum(piece).wait_send()
        x_sum(piece).wait_recv()


def exchange(pre_act, grad_out, weight):
    tokens, cols = pre_act.shape
    block, width = grad_out.shape
    units = cols // 2
    bf16, f32 = jnp.bfloat16, jnp.float32
    vmem = pl.BlockSpec(memory_space=pltpu.VMEM)
    in_hbm = pl.BlockSpec(memory_space=pltpu.HBM)
    dma = pltpu.SemaphoreType.DMA
    return pl.pallas_call(
        exchange_kernel,
        out_shape=(
            pltpu.VMEM(weight.shape, bf16),
            pltpu.VMEM((2, tokens, units), bf16),
            pltpu.VMEM((tokens, cols), f32),
        ),
        in_specs=[in_hbm, in_hbm, in_hbm],
        out_specs=(vmem, vmem, vmem),
        scratch_shapes=[
            pltpu.VMEM(weight.shape, bf16),
            pltpu.VMEM((tokens, cols), bf16),
            pltpu.VMEM((2, tokens, width), bf16),
            pltpu.VMEM((2, 4, units, tokens), bf16),
            pltpu.VMEM((units, tokens), bf16),
            pltpu.VMEM((8, tokens, units), f32),
            pltpu.VMEM((2, 4, 4, tokens // 2, units), bf16),
            pltpu.VMEM((14, tokens // 2, units), bf16),
            dma((3,)),
            dma((7,)),
            dma((7,)),
            dma((4,)),
            dma((4,)),
            dma((2, 4, 3)),
            dma((2, 4, 3)),
            dma((12,)),
            dma((2, 4, 4)),
        ],
        compiler_params=pltpu.CompilerParams(
            collective_id=0, has_side_effects=True, vmem_limit_bytes=52 * 1024 * 1024
        ),
        name="exchange",
    )(pre_act, grad_out, weight)


def finish_kernel(weight_grad_ref, sums_ref, slope_ref, pre_grad_out, weight_grad_out, pre_grad, sem):
    own = lax.axis_index("gx")
    copies = []
    count = weight_grad_ref.shape[0] // 4
    for q in range(4):
        span = pl.ds(q * count, count)
        copies.append(
            pltpu.make_async_copy(weight_grad_ref.at[span, :], weight_grad_out.at[span, :], sem.at[q])
        )
        copies[-1].start()
    group = 256
    half = group // 2
    line = lax.broadcasted_iota(jnp.int32, (group, group), 0)
    lane = lax.broadcasted_iota(jnp.int32, (group, group), 1)
    target = jnp.where(line < half, 2 * line + own, 2 * (line - half) + 1 - own)
    select = jnp.where(lane == target, 1.0, 0.0).astype(jnp.bfloat16)
    for q in range(slope_ref.shape[1] // group):
        span = slice(q * group, (q + 1) * group)
        pair = jnp.concatenate(
            [sums_ref[0, :, q * half : (q + 1) * half], sums_ref[1, :, q * half : (q + 1) * half]], axis=1
        )
        total = jnp.dot(pair, select, preferred_element_type=jnp.float32)
        pre_grad[:, span] = (total * slope_ref[:, span]).astype(jnp.bfloat16)
        copies.append(
            pltpu.make_async_copy(pre_grad.at[:, span], pre_grad_out.at[:, span], sem.at[4 + q])
        )
        copies[-1].start()
    for copy in copies:
        copy.wait()


def with_kernel(pre_act, grad_out, weight):
    weight_grad, sums, slope = exchange(pre_act, grad_out, weight[:, 0, :])
    vmem = pl.BlockSpec(memory_space=pltpu.VMEM)
    anywhere = pl.BlockSpec(memory_space=pl.ANY)
    pre_grad, weight_grad = pl.pallas_call(
        finish_kernel,
        out_shape=(
            pltpu.HBM(pre_act.shape, jnp.bfloat16),
            pltpu.HBM(weight_grad.shape, jnp.bfloat16),
        ),
        in_specs=[anywhere, vmem, vmem],
        out_specs=(anywhere, anywhere),
        scratch_shapes=[pltpu.VMEM(pre_act.shape, jnp.bfloat16), pltpu.SemaphoreType.DMA((4 + pre_act.shape[1] // 256,))],
        compiler_params=pltpu.CompilerParams(vmem_limit_bytes=8 * 1024 * 1024),
        name="finish",
    )(weight_grad, sums, slope)
    return (pre_grad, weight_grad[:, None, :])


def with_collectives(pre_act, grad_out, weight):
    groups = lax.axis_size("gx")
    tokens, cols = pre_act.shape
    value, slope = gelu_parts(pre_act.astype(jnp.float32))
    split = value.astype(jnp.bfloat16).reshape(tokens, cols // groups, groups).transpose(2, 0, 1)
    hidden = lax.all_to_all(split, "gx", 0, 0, tiled=True)
    hidden = lax.all_gather(hidden, "gz", axis=2, tiled=True)
    hidden = hidden.reshape(groups * tokens, -1)
    grad_rows = lax.all_gather(grad_out, ("gx", "gy"), axis=0, tiled=True)
    partial = jnp.einsum("pd,rd->pr", grad_rows, weight[:, 0, :], preferred_element_type=jnp.float32)
    summed = lax.psum_scatter(partial.astype(jnp.bfloat16), "gz", scatter_dimension=1, tiled=True)
    summed = lax.all_to_all(summed.reshape(groups, tokens, -1), "gx", 0, 0, tiled=True)
    summed = summed.transpose(1, 2, 0).reshape(tokens, cols).astype(jnp.float32)
    pre_grad = (summed * slope).astype(jnp.bfloat16)
    weight_grad = jnp.einsum("pr,pd->rd", hidden, grad_rows, preferred_element_type=jnp.float32)
    return (pre_grad, weight_grad.astype(jnp.bfloat16)[:, None, :])


def solution(mesh):
    sizes = tuple(mesh.shape[name] for name in ("gx", "gy", "gz"))
    placed = (P("gx", ("gy", "gz")), P(("gx", "gy"), "gz"), P("gy", "gx", "gz"))
    return jax.shard_map(
        with_kernel if sizes == (2, 4, 4) else with_collectives,
        mesh=mesh,
        in_specs=placed,
        out_specs=(P("gx", ("gy", "gz")), P("gy", "gx", "gz")),
        check_vma=False,
    )
```
